128 devices in a mesh: gx: 8 (over z, core), gy: 16 (over x, y).
Axes of the slice: x: 4, y: 4, z: 4, core: 2. Of those that a mesh axis runs over, the one named last changes fastest.
Arguments:
- sensitivity: float32 [3, 1048576], P(None, ('gx', 'gy')), may hold values from -24 to 24
- node_weight: float32 [1048576], P(('gx', 'gy')), may hold values from 0.05 to 0.5
- dest_device: int32 [1048576, 1], P(('gx', 'gy')), may hold values from 0 to 127; in each aligned block of 8192 rows (0 to 8191, 8192 to 16383, ...) at most 128 rows name the same one
- dest_cell: int32 [1048576], P(('gx', 'gy')), may hold values from 0 to 131071
- box_owner: int32 [1048576, 1], P(('gx', 'gy')), may hold values from 0 to 127; in each aligned block of 8192 rows (0 to 8191, 8192 to 16383, ...) at most 128 rows name the same one
- box_slot: int32 [1048576], P(('gx', 'gy')), may hold values from 0 to 63
- stiffness: float32 [128, 512, 256], P('gx', 'gy'), may hold values from 0.5 to 2
- anchor: float32 [3, 128, 512, 256], P(None, 'gx', 'gy'), may hold values from 3 to 6
- coupling: float32 [9, 128, 512, 256], P(None, 'gx', 'gy'), may hold values from -1 to 1
Outputs:
- adjoint: float32 [3, 128, 512, 256], P(None, 'gx', 'gy')
- box_gradient: float32 [3, 8192], P(None, ('gx', 'gy'))
The draws below stay inside these ranges and needn't reach their ends.
Inputs may be any that keep to these rules, and one draw needn't show every extreme that they name: `dest_device`: among the rows of one device, no deformation device is named more than 128 times, and in some device's rows one is named exactly 128 times. `box_owner`: among the rows of one device, no owner is named more than 128 times, and in some device's rows one is named exactly 128 times.
All inputs are finite; a program needn't handle non-finite values.
Results may differ from the reference program's by a relative error of at most 0.0003.
Values sent between devices are 32-bit elements; how exact they have to be, the bound alone decides.
No kernel may reach another device: no remote copies, remote signals or barrier semaphores. Data moves between devices by JAX's collectives and lax.ppermute only.
A program may use at most 192 MiB of HBM per device.

```python
import math
import jax
import jax.numpy as jnp
import numpy as np

CX = 16
CY = 32
CZ = 256
SR_DEV = 8192
BOX_DEV = 64
SWEEPS = 4
CAP = 128
NX = 128
NY = 512
NZ = 256
ROWS = 1048576
BOXES = 8192
N_GX = 8
N_GY = 16


def set_ends(result, own_key, smallest, high):
    place = [jax.random.randint(jax.random.fold_in(own_key, axis), (), 0, length) for axis, length in enumerate(result.shape)]
    longest = result.shape.index(max(result.shape))
    neighbour = place[:longest] + [(place[longest] + 1) % result.shape[longest]] + place[longest + 1:]
    return result.at[tuple(place)].set(smallest).at[tuple(neighbour)].set(high)


def levels(rng, shape, cuts, least, high):
    def one(position, parts):
        heights = jax.random.uniform(jax.random.fold_in(jax.random.fold_in(rng, 6), position), (parts,), jnp.float32, least / len(cuts), high / len(cuts))
        return jnp.repeat(jnp.exp(heights), shape[position] // parts).reshape((-1,) + (1,) * (len(shape) - position - 1))

    gain = one(*cuts[0])
    for cut in cuts[1:]:
        gain = gain * one(*cut)
    return gain


def assign_block(own_key, own, number, rows, number_of, top, most, lean):
    sequence = jax.random.permutation(own_key, number_of)
    heavy_load, common = load_shares(number_of, rows * top, most, lean, True), load_shares(number_of, rows * top, most, lean, False)
    places = jnp.arange(number_of)

    def named(tallies, rotation):
        used = int((tallies > 0).sum())
        fixed = max(1, used // 4)
        moved = fixed + (places - fixed + rotation * (used - fixed)) % max(1, number_of - fixed)
        return jnp.zeros((number_of,), jnp.int32).at[sequence[jnp.where(places < fixed, places, moved)]].set(jnp.asarray(tallies, jnp.int32))

    tallies = jnp.where(number % 4 == 0, named(heavy_load, number // 4), named(common, number - number // 4 - 1))
    mixed = jax.random.permutation(jax.random.fold_in(own, 3), number_of)
    donor, receiver = mixed[0:number_of // 2 * 2:2], mixed[1:number_of // 2 * 2:2]
    slack = jnp.minimum(tallies[donor] - 1, most - tallies[receiver]) // 2
    slack = jnp.where((donor == sequence[0]) | (receiver == sequence[0]) | (tallies[receiver] == 0), 0, jnp.maximum(slack, 0))
    moved = jax.random.randint(jax.random.fold_in(own, 4), (number_of // 2,), 0, 1 << 20) % (slack + 1)
    tallies = tallies.at[donor].add(-moved).at[receiver].add(moved)
    labels = jnp.searchsorted(jnp.cumsum(tallies), jnp.arange(rows * top), side="right").astype(jnp.int32)
    grid = labels.reshape(top, rows).T
    grid = grid[jax.random.permutation(jax.random.fold_in(own, 1), rows)]
    rotation = jax.random.randint(jax.random.fold_in(own, 2), (rows, 1), 0, top)
    return jnp.take_along_axis(grid, (jnp.arange(top)[None, :] + rotation) % top, axis=1)


def load_shares(count, total, limit, lean, full):
    loads = [(1 << 20) // math.isqrt(grade ** lean) + 1 for grade in range(1, count + 1)]
    largest = limit if full else min(limit, max(-(-total // count), total * loads[0] // sum(loads)))
    least = 1 if total - largest >= count - 1 else 0
    counts, surplus = [largest] + [least] * (count - 1), total - largest - least * (count - 1)
    while surplus > 0:
        candidates = [i for i in range(1, count) if counts[i] < largest] or [i for i in range(1, count) if counts[i] < limit]
        mass, left = sum([loads[i] for i in candidates]), surplus
        for i in candidates:
            extra = min(limit - counts[i], max(1, left * loads[i] // mass), surplus)
            counts[i] = counts[i] + extra
            surplus = surplus - extra
    return np.array(counts)


def noise(rng, shape, width, bound, split=(), dtype=jnp.bfloat16):
    array = jax.random.normal(rng, shape, jnp.float32) * width
    if len(split) > 0:
        array = levels(rng, shape, split, -0.22, 0.18) * array
    return jnp.clip(array, min=-bound, max=bound).astype(dtype)


def setup_inputs(seed: int = 0) -> dict:
    keys = jax.random.split(jax.random.key(seed), 10)
    sensitivity = noise(keys[0], (3, ROWS), 4.0, 24.0, ((1, 128),), jnp.float32)
    node_weight = jnp.clip(0.05 + 0.45 * jax.random.uniform(keys[1], (ROWS,), jnp.float32) ** levels(keys[1], (ROWS,), ((0, 128),), -0.2, 0.2), 0.05, 0.5)
    dest_device_keys = jax.random.split(jax.random.fold_in(keys[2], 1), ROWS // SR_DEV)
    dest_device_turns = jax.random.permutation(jax.random.fold_in(keys[2], 3), ROWS // SR_DEV)
    dest_device = jax.vmap(lambda own, number: assign_block(jax.random.fold_in(keys[2], 2), own, number, SR_DEV, N_GX * N_GY, 1, CAP, 2))(dest_device_keys, dest_device_turns).reshape((ROWS, 1))
    dest_cell = set_ends(jax.random.randint(keys[3], (ROWS,), 0, CX * CY * CZ), jax.random.fold_in(keys[3], 1), 0, (CX * CY * CZ) - 1).astype(jnp.int32)
    box_owner_keys = jax.random.split(jax.random.fold_in(keys[4], 1), ROWS // SR_DEV)
    box_owner_turns = jax.random.permutation(jax.random.fold_in(keys[4], 3), ROWS // SR_DEV)
    box_owner = jax.vmap(lambda own, number: assign_block(jax.random.fold_in(keys[4], 2), own, number, SR_DEV, N_GX * N_GY, 1, CAP, 1))(box_owner_keys, box_owner_turns).reshape((ROWS, 1))
    box_slot = set_ends(jax.random.randint(keys[5], (ROWS,), 0, BOX_DEV), jax.random.fold_in(keys[5], 1), 0, BOX_DEV - 1).astype(jnp.int32)
    stiffness = jnp.clip(jnp.exp(math.log(2.0) - 1.3862944 * jax.random.uniform(keys[6], (NX, NY, NZ), jnp.float32) ** levels(keys[6], (NX, NY, NZ), ((0, 8), (1, 16)), -0.2, 0.2)), 0.5, 2.0)
    anchor = jnp.clip(jnp.exp(math.log(6.0) - 0.6931472 * jax.random.uniform(keys[7], (3, NX, NY, NZ), jnp.float32) ** levels(keys[7], (3, NX, NY, NZ), ((1, 8), (2, 16)), -0.2, 0.2)), 3.0, 6.0)
    coupling = jnp.clip(jax.random.uniform(keys[8], (9, NX, NY, NZ), jnp.float32, -1.0, 1.0) * levels(keys[8], (9, NX, NY, NZ), ((1, 8), (2, 16)), -0.4, 0.0), -1.0, 1.0)
    return dict(sensitivity=sensitivity, node_weight=node_weight, dest_device=dest_device, dest_cell=dest_cell, box_owner=box_owner, box_slot=box_slot, stiffness=stiffness, anchor=anchor, coupling=coupling)


def neighbour_sum(padded):
    z_padded = jnp.pad(padded, ((0, 0), (0, 0), (0, 0), (1, 1)))
    middle = z_padded[:, 1:-1, 1:-1, :]
    total = z_padded[:, 2:, 1:-1, 1:-1] + z_padded[:, :-2, 1:-1, 1:-1]
    total = total + z_padded[:, 1:-1, 2:, 1:-1] + z_padded[:, 1:-1, :-2, 1:-1]
    return total + middle[..., 2:] + middle[..., :-2]


def apply_transposed(field, weighted_pad, stiff, anchor, coupling):
    blocks = coupling.reshape((3, 3) + coupling.shape[1:])
    mixing = jnp.sum(blocks * field[:, None], axis=0)
    return 6.0 * stiff[None] * field - neighbour_sum(weighted_pad) + mixing + anchor * field


def reference(sensitivity, node_weight, dest_device, dest_cell, box_owner, box_slot, stiffness, anchor, coupling):
    target = dest_device[:, 0]
    local_cell = dest_cell
    x_cell = (target // N_GY) * CX + local_cell // (CY * CZ)
    y_cell = (target % N_GY) * CY + (local_cell // CZ) % CY
    z_cell = local_cell % CZ
    flat_ids = ((x_cell * NY + y_cell) * NZ + z_cell).astype(jnp.int32)
    load = jnp.zeros((3, NX * NY * NZ), jnp.float32).at[:, flat_ids].add(sensitivity)
    load = load.reshape(3, NX, NY, NZ)
    diagonal = 6.0 * stiffness[None] + anchor + jnp.stack([coupling[0], coupling[4], coupling[8]])
    adjoint = jnp.zeros((3, NX, NY, NZ), jnp.float32)
    for sweep_idx in range(SWEEPS):
        weighted = jnp.pad(stiffness[None] * adjoint, ((0, 0), (1, 1), (1, 1), (0, 0)))
        applied = apply_transposed(adjoint, weighted, stiffness, anchor, coupling)
        adjoint = adjoint + (load - applied) / diagonal
    flat_field = adjoint.reshape(3, NX * NY * NZ)
    row_gradient = node_weight[None] * flat_field[:, flat_ids]
    box_ids = (box_owner[:, 0] * BOX_DEV + box_slot).astype(jnp.int32)
    box_gradient = jax.ops.segment_sum(row_gradient.T, box_ids, num_segments=BOXES).T
    return adjoint, box_gradient
```

```python
import jax
import jax.numpy as jnp
from jax import lax
from jax.experimental import pallas as pl
from jax.experimental.pallas import tpu as pltpu
from jax.sharding import PartitionSpec as P

BOX_DEV = 64
SWEEPS = 4
AXES = ("gx", "gy")
STEP_ROWS = 512
MIB = 1024 * 1024


def dot_last(left, right):
    return lax.dot_general(
        left, right, (((1,), (1,)), ((), ())), preferred_element_type=jnp.float32
    )


def halves(values):
    high = values.astype(jnp.bfloat16).astype(jnp.float32)
    return high, values - high


def places(height, width):
    return lax.broadcasted_iota(jnp.int32, (height, width), 0)


def marked(mask, row):
    return jnp.where(mask, row, 0.0).astype(jnp.bfloat16)


def pack_kernel(sens, weight, device, cell, owner, slot, rows, tags, upper, left, right, total):
    devices, _, capacity = rows.shape
    step = upper.shape[0]
    half_cells = float(2**16)
    before = lax.broadcasted_iota(jnp.int32, (step, step), 0)
    after = lax.broadcasted_iota(jnp.int32, (step, step), 1)
    upper[...] = marked(before < after, 1.0)
    total[...] = jnp.zeros_like(total)

    def chunk(i, base):
        at = pl.ds(pl.multiple_of(i * step, step), step)
        named = places(devices, step) == device[:, at]
        ones = jnp.where(named, 1.0, 0.0)
        left[:, :step] = ones.astype(jnp.bfloat16)
        left[:, step:] = ones.astype(jnp.bfloat16)
        within = jnp.dot(left[:, :step], upper[...], preferred_element_type=jnp.float32)
        rank = jnp.sum(jnp.where(named, within + base, 0.0), axis=0, keepdims=True)
        here = places(capacity, step) == rank.astype(jnp.int32)
        own_cell = cell[:, at]
        pairs = [halves(sens[k : k + 1, at]) for k in range(3)]
        pairs.append(
            (
                ((own_cell >> 8) << 8).astype(jnp.float32) - half_cells,
                (own_cell & 255).astype(jnp.float32),
            )
        )
        pairs.append(halves(weight[:, at]))
        pairs.append(((owner[:, at] * BOX_DEV).astype(jnp.float32), slot[:, at].astype(jnp.float32)))
        for p, (high, low) in enumerate(pairs):
            band = slice(p * capacity, (p + 1) * capacity)
            right[band, :step] = marked(here, high)
            right[band, step:] = marked(here, low)
        total[...] += dot_last(left[...], right[...])
        return base + jnp.sum(ones, axis=1, keepdims=True)

    lax.fori_loop(0, sens.shape[1] // step, chunk, jnp.zeros((devices, 1), jnp.float32))
    for p in range(4):
        rows[:, p, :] = total[:, p * capacity : (p + 1) * capacity]
    for p in range(2):
        tags[:, p, :] = total[:, (4 + p) * capacity : (5 + p) * capacity]


def pack(sensitivity, weight, device, cell, owner, slot, devices):
    count = sensitivity.shape[1]
    capacity = 2 * count // devices
    return pl.pallas_call(
        pack_kernel,
        out_shape=(
            jax.ShapeDtypeStruct((devices, 4, capacity), jnp.float32),
            jax.ShapeDtypeStruct((devices, 2, capacity), jnp.float32),
        ),
        scratch_shapes=[
            pltpu.VMEM((STEP_ROWS, STEP_ROWS), jnp.bfloat16),
            pltpu.VMEM((devices, 2 * STEP_ROWS), jnp.bfloat16),
            pltpu.VMEM((6 * capacity, 2 * STEP_ROWS), jnp.bfloat16),
            pltpu.VMEM((devices, 6 * capacity), jnp.float32),
        ],
        compiler_params=pltpu.CompilerParams(vmem_limit_bytes=16 * MIB),
        name="pack_rows",
    )(sensitivity, weight, device, cell, owner, slot)


def cell_parts(row):
    cell = row.astype(jnp.int32) + 2**16
    return cell >> 8, cell & 255


def scatter_kernel(rows, load, left, right):
    height, depth = load.shape[1:]
    sources, _, width = rows.shape
    group = left.shape[1] // 2 // width
    step = group * width
    load[...] = jnp.zeros_like(load)

    def chunk(i, _):
        for q in range(group):
            source = i * group + q
            at = slice(q * width, (q + 1) * width)
            low_at = slice(step + q * width, step + (q + 1) * width)
            line, place = cell_parts(rows[source, 3:4, :])
            hot = marked(places(height, width) == line, 1.0)
            left[:, at] = hot
            left[:, low_at] = hot
            there = places(depth, width) == place
            for k in range(3):
                high, low = halves(rows[source, k : k + 1, :])
                band = slice(k * depth, (k + 1) * depth)
                right[band, at] = marked(there, high)
                right[band, low_at] = marked(there, low)
        for k in range(3):
            load[k] += dot_last(left[...], right[k * depth : (k + 1) * depth, :])
        return 0

    lax.fori_loop(0, sources // group, chunk, 0)


def scatter(rows, height, depth):
    return pl.pallas_call(
        scatter_kernel,
        out_shape=jax.ShapeDtypeStruct((3, height, depth), jnp.float32),
        scratch_shapes=[
            pltpu.VMEM((height, 2 * STEP_ROWS), jnp.bfloat16),
            pltpu.VMEM((3 * depth, 2 * STEP_ROWS), jnp.bfloat16),
        ],
        compiler_params=pltpu.CompilerParams(vmem_limit_bytes=24 * MIB),
        name="scatter_rows",
    )(rows)


def sweep_kernel(last, field, load, inverse, stiff, coupling, west, east, south, north, *outs):
    _, size_x, size_y, size_z = field.shape
    padded = outs[-1]
    result = outs[0]
    padded[:, 0] = west[...]
    padded[:, size_x + 1] = east[...]
    for x in range(size_x):
        for k in range(3):
            padded[k, x + 1] = stiff[x] * field[k, x]
    row = lax.broadcasted_iota(jnp.int32, (size_y, size_z), 0)
    column = lax.broadcasted_iota(jnp.int32, (size_y, size_z), 1)
    for x in range(size_x):
        own = [field[k, x] for k in range(3)]
        for k in range(3):
            middle = padded[k, x + 1]
            total = load[k, x] + padded[k, x] + padded[k, x + 2]
            total = total + jnp.where(row == 0, south[k, x : x + 1], pltpu.roll(middle, 1, 0))
            total = total + jnp.where(
                row == size_y - 1, north[k, x : x + 1], pltpu.roll(middle, size_y - 1, 0)
            )
            total = total + jnp.where(column == 0, 0.0, pltpu.roll(middle, 1, 1))
            total = total + jnp.where(
                column == size_z - 1, 0.0, pltpu.roll(middle, size_z - 1, 1)
            )
            for j in range(3):
                if j != k:
                    total = total - coupling[3 * j + k, x] * own[j]
            fresh = total * inverse[k, x]
            result[k, x] = fresh
            if not last:
                head_x, tail_x, head_y, tail_y = outs[1:5]
                moved = stiff[x] * fresh
                if x == 0:
                    head_x[k] = moved
                if x == size_x - 1:
                    tail_x[k] = moved
                head_y[k, x : x + 1] = moved[:1]
                tail_y[k, x : x + 1] = moved[size_y - 1 :]


def sweep(last, field, load, inverse, stiff, coupling, halo):
    _, size_x, size_y, size_z = field.shape
    shapes = [field.shape]
    if not last:
        shapes += [(3, size_y, size_z)] * 2 + [(3, size_x, size_z)] * 2

    def kernel(*refs):
        sweep_kernel(last, *refs)

    return pl.pallas_call(
        kernel,
        out_shape=[jax.ShapeDtypeStruct(shape, jnp.float32) for shape in shapes],
        scratch_shapes=[pltpu.VMEM((3, size_x + 2, size_y, size_z), jnp.float32)],
        compiler_params=pltpu.CompilerParams(vmem_limit_bytes=24 * MIB),
        name="sweep_cells",
    )(field, load, inverse, stiff, coupling, *halo)


def exchange(head_x, tail_x, head_y, tail_y):
    def shifted(face, axis, up):
        pairs = [(i, i + 1) if up else (i + 1, i) for i in range(lax.axis_size(axis) - 1)]
        return lax.ppermute(face, axis, pairs)

    return (
        shifted(tail_x, "gx", True),
        shifted(head_x, "gx", False),
        shifted(tail_y, "gy", True),
        shifted(head_y, "gy", False),
    )


def gather_kernel(field, rows, tags, boxes, turned, hot, left, right, total):
    height, depth = field.shape[1:]
    sources, _, width = rows.shape
    group = hot.shape[1] // width
    step = group * width
    for k in range(3):
        high, low = halves(field[k].T)
        turned[k * depth : (k + 1) * depth, :height] = high.astype(jnp.bfloat16)
        turned[k * depth : (k + 1) * depth, height:] = low.astype(jnp.bfloat16)
    total[...] = jnp.zeros_like(total)
    right[...] = jnp.zeros_like(right)

    def chunk(i, _):
        for q in range(group):
            line, _ = cell_parts(rows[i * group + q, 3:4, :])
            ones = marked(places(height, width) == line, 1.0)
            hot[:height, q * width : (q + 1) * width] = ones
            hot[height:, q * width : (q + 1) * width] = ones
        parts = [
            jnp.dot(
                turned[k * depth : (k + 1) * depth, :], hot[...], preferred_element_type=jnp.float32
            )
            for k in range(3)
        ]
        for q in range(group):
            source = i * group + q
            at = slice(q * width, (q + 1) * width)
            low_at = slice(step + q * width, step + (q + 1) * width)
            _, place = cell_parts(rows[source, 3:4, :])
            there = places(depth, width) == place
            weight = tags[source, 0:1, :]
            box = tags[source, 1:2, :].astype(jnp.int32)
            owned = marked(places(left.shape[0], width) == box // BOX_DEV, 1.0)
            left[:, at] = owned
            left[:, low_at] = owned
            inside = places(BOX_DEV, width) == box % BOX_DEV
            for k in range(3):
                picked = jnp.sum(jnp.where(there, parts[k][:, at], 0.0), axis=0, keepdims=True)
                high, low = halves(picked * weight)
                band = slice(k * BOX_DEV, (k + 1) * BOX_DEV)
                right[band, at] = marked(inside, high)
                right[band, low_at] = marked(inside, low)
        total[...] += dot_last(left[...], right[...])
        return 0

    lax.fori_loop(0, sources // group, chunk, 0)
    for p in range(2):
        boxes[:, p, :] = total[:, p * 128 : (p + 1) * 128]


def gather(field, rows, tags):
    height, depth = field.shape[1:]
    devices = rows.shape[0]
    return pl.pallas_call(
        gather_kernel,
        out_shape=jax.ShapeDtypeStruct((devices, 2, 128), jnp.float32),
        scratch_shapes=[
            pltpu.VMEM((3 * depth, 2 * height), jnp.bfloat16),
            pltpu.VMEM((2 * height, STEP_ROWS), jnp.bfloat16),
            pltpu.VMEM((devices, 2 * STEP_ROWS), jnp.bfloat16),
            pltpu.VMEM((4 * BOX_DEV, 2 * STEP_ROWS), jnp.bfloat16),
            pltpu.VMEM((devices, 4 * BOX_DEV), jnp.float32),
        ],
        compiler_params=pltpu.CompilerParams(vmem_limit_bytes=24 * MIB),
        name="gather_rows",
    )(field, rows, tags)


def swapped(blocks):
    return lax.all_to_all(blocks, AXES, split_axis=0, concat_axis=0, tiled=True)


def body(
    sensitivity,
    node_weight,
    dest_device,
    dest_cell,
    box_owner,
    box_slot,
    stiffness,
    anchor,
    coupling,
):
    devices = lax.axis_size("gx") * lax.axis_size("gy")
    count = sensitivity.shape[1]
    size_x, size_y, size_z = stiffness.shape
    lane = lambda values: values.reshape(1, count)
    rows, tags = pack(
        sensitivity,
        lane(node_weight),
        lane(dest_device),
        lane(dest_cell),
        lane(box_owner),
        lane(box_slot),
        devices,
    )
    rows = swapped(rows)
    tags = swapped(tags)
    diagonal = 6.0 * stiffness[None] + anchor + jnp.stack([coupling[0], coupling[4], coupling[8]])
    inverse = 1.0 / diagonal
    load = scatter(rows, size_x * size_y, size_z).reshape(3, size_x, size_y, size_z)
    field = load * inverse
    moved = stiffness[None] * field
    faces = (moved[:, 0], moved[:, -1], moved[:, :, 0], moved[:, :, -1])
    for turn in range(1, SWEEPS):
        last = turn == SWEEPS - 1
        field, *faces = sweep(
            last, field, load, inverse, stiffness, coupling, exchange(*faces)
        )
    partial = gather(field.reshape(3, size_x * size_y, size_z), rows, tags)
    summed = jnp.sum(swapped(partial), axis=0).reshape(4, BOX_DEV)
    return (field, summed[:3])


def solution(mesh):
    placed = (
        P(None, AXES),
        P(AXES),
        P(AXES, None),
        P(AXES),
        P(AXES, None),
        P(AXES),
        P("gx", "gy", None),
        P(None, "gx", "gy", None),
        P(None, "gx", "gy", None),
    )
    return jax.shard_map(
        body,
        mesh=mesh,
        in_specs=placed,
        out_specs=(P(None, "gx", "gy", None), P(None, AXES)),
        check_vma=False,
    )
```

```python
import jax
import jax.numpy as jnp
from jax import lax
from jax.experimental import pallas as pl
from jax.experimental.pallas import tpu as pltpu
from jax.sharding import PartitionSpec as P

BOX_DEV = 64
SWEEPS = 4
AXES = ("gx", "gy")
STEP_ROWS = 512
WINDOW = 32
CELL_SHIFT = 257
MIB = 1024 * 1024


def dot_last(left, right):
    return lax.dot_general(
        left, right, (((1,), (1,)), ((), ())), preferred_element_type=jnp.float32
    )


def halves(values):
    high = values.astype(jnp.bfloat16).astype(jnp.float32)
    return high, values - high


def places(height, width):
    return lax.broadcasted_iota(jnp.int32, (height, width), 0)


def marked(mask, row):
    return jnp.where(mask, row, 0.0).astype(jnp.bfloat16)


def pack_kernel(sens, weight, device, cell, owner, slot, rows, upper, left, right, total):
    devices, _, capacity = rows.shape
    step = upper.shape[0]
    before = lax.broadcasted_iota(jnp.int32, (step, step), 0)
    after = lax.broadcasted_iota(jnp.int32, (step, step), 1)
    upper[...] = marked(before < after, 1.0)
    total[...] = jnp.zeros_like(total)

    def chunk(i, base):
        at = pl.ds(pl.multiple_of(i * step, step), step)
        named = places(devices, step) == device[:, at]
        ones = jnp.where(named, 1.0, 0.0)
        left[:, :step] = ones.astype(jnp.bfloat16)
        left[:, step:] = ones.astype(jnp.bfloat16)
        within = jnp.dot(left[:, :step], upper[...], preferred_element_type=jnp.float32)
        rank = jnp.sum(jnp.where(named, within + base, 0.0), axis=0, keepdims=True)
        here = places(capacity, step) == rank.astype(jnp.int32)
        own_cell = cell[:, at]
        pairs = [halves(sens[k : k + 1, at]) for k in range(3)]
        pairs.append(
            (
                (((own_cell >> 9) + 1) << 9).astype(jnp.float32),
                ((own_cell & 511) + (CELL_SHIFT - 512)).astype(jnp.float32),
            )
        )
        pairs.append(halves(weight[:, at]))
        pairs.append(((owner[:, at] * BOX_DEV).astype(jnp.float32), slot[:, at].astype(jnp.float32)))
        for p, (high, low) in enumerate(pairs):
            band = slice(p * capacity, (p + 1) * capacity)
            right[band, :step] = marked(here, high)
            right[band, step:] = marked(here, low)
        total[...] += dot_last(left[...], right[...])
        return base + jnp.sum(ones, axis=1, keepdims=True)

    lax.fori_loop(0, sens.shape[1] // step, chunk, jnp.zeros((devices, 1), jnp.float32))
    for p in range(6):
        rows[:, p, :] = total[:, p * capacity : (p + 1) * capacity]
    for p in range(6, 8):
        rows[:, p, :] = jnp.zeros((devices, capacity), jnp.float32)


def pack(sensitivity, weight, device, cell, owner, slot, devices):
    count = sensitivity.shape[1]
    capacity = 2 * count // devices
    return pl.pallas_call(
        pack_kernel,
        out_shape=jax.ShapeDtypeStruct((devices, 8, capacity), jnp.float32),
        scratch_shapes=[
            pltpu.VMEM((STEP_ROWS, STEP_ROWS), jnp.bfloat16),
            pltpu.VMEM((devices, 2 * STEP_ROWS), jnp.bfloat16),
            pltpu.VMEM((6 * capacity, 2 * STEP_ROWS), jnp.bfloat16),
            pltpu.VMEM((devices, 6 * capacity), jnp.float32),
        ],
        compiler_params=pltpu.CompilerParams(vmem_limit_bytes=16 * MIB),
        name="pack_rows",
    )(sensitivity, weight, device, cell, owner, slot)


def windows(ends, i):
    first = jnp.maximum(ends[0, i] >> 8, 0)
    start = first & ~7
    return start, (jnp.maximum((ends[1, i] >> 8) + WINDOW - start, 0)) // WINDOW


def scatter_kernel(ends, cells, one, two, three, load, left, right):
    height, depth = load.shape[1:]
    lines, width = cells.shape
    half = depth // 2
    group = STEP_ROWS // width
    step = STEP_ROWS
    load[...] = jnp.zeros_like(load)

    def chunk(i, _):
        for q in range(group):
            row = pl.ds(i * group + q, 1)
            place = cells[row, :] & (half - 1)
            there = places(half, width) == place
            for k, sens in enumerate((one, two, three)):
                high, low = halves(sens[row, :])
                band = slice(k * half, (k + 1) * half)
                right[band, q * width : (q + 1) * width] = marked(there, high)
                right[band, step + q * width : step + (q + 1) * width] = marked(there, low)
        start, count = windows(ends, i)

        def window(w, _):
            least = start + w * WINDOW
            base = pl.multiple_of(jnp.minimum(least, height - WINDOW), 8)
            for q in range(group):
                cell = cells[pl.ds(i * group + q, 1), :]
                hot = marked(places(2 * WINDOW, width) == window_place(cell, least, base), 1.0)
                left[:, q * width : (q + 1) * width] = hot
                left[:, step + q * width : step + (q + 1) * width] = hot
            sums = dot_last(left[...], right[...])
            for k in range(3):
                for side in range(2):
                    at = (k, pl.ds(base, WINDOW), slice(side * half, (side + 1) * half))
                    load[at] += sums[
                        side * WINDOW : (side + 1) * WINDOW, k * half : (k + 1) * half
                    ]
            return 0

        lax.fori_loop(0, count, window, 0)
        return 0

    lax.fori_loop(0, lines // group, chunk, 0)


def window_place(cell, least, base):
    line = cell >> 8
    place = ((cell >> 7) & 1) * WINDOW + line - base
    inside = (line >= least) & (line < base + WINDOW)
    return jnp.where(inside, place, -1)


def scatter(ends, cells, values, height, depth):
    vmem = pl.BlockSpec(memory_space=pltpu.VMEM)
    return pl.pallas_call(
        scatter_kernel,
        in_specs=[pl.BlockSpec(memory_space=pltpu.SMEM)] + [vmem] * 4,
        out_specs=vmem,
        out_shape=jax.ShapeDtypeStruct((3, height, depth), jnp.float32),
        scratch_shapes=[
            pltpu.VMEM((2 * WINDOW, 2 * STEP_ROWS), jnp.bfloat16),
            pltpu.VMEM((3 * depth // 2, 2 * STEP_ROWS), jnp.bfloat16),
        ],
        compiler_params=pltpu.CompilerParams(vmem_limit_bytes=16 * MIB),
        name="scatter_rows",
    )(ends, cells, *values)


def sweep_kernel(last, field, load, inverse, stiff, coupling, west, east, south, north, *outs):
    _, size_x, size_y, size_z = field.shape
    padded = outs[-1]
    result = outs[0]
    padded[:, 0] = west[...]
    padded[:, size_x + 1] = east[...]
    for x in range(size_x):
        for k in range(3):
            padded[k, x + 1] = stiff[x] * field[k, x]
    row = lax.broadcasted_iota(jnp.int32, (size_y, size_z), 0)
    column = lax.broadcasted_iota(jnp.int32, (size_y, size_z), 1)
    for x in range(size_x):
        own = [field[k, x] for k in range(3)]
        for k in range(3):
            middle = padded[k, x + 1]
            total = load[k, x] + padded[k, x] + padded[k, x + 2]
            total = total + jnp.where(row == 0, south[k, x : x + 1], pltpu.roll(middle, 1, 0))
            total = total + jnp.where(
                row == size_y - 1, north[k, x : x + 1], pltpu.roll(middle, size_y - 1, 0)
            )
            total = total + jnp.where(column == 0, 0.0, pltpu.roll(middle, 1, 1))
            total = total + jnp.where(
                column == size_z - 1, 0.0, pltpu.roll(middle, size_z - 1, 1)
            )
            for j in range(3):
                if j != k:
                    total = total - coupling[3 * j + k, x] * own[j]
            fresh = total * inverse[k, x]
            result[k, x] = fresh
            if not last:
                head_x, tail_x, head_y, tail_y = outs[1:5]
                moved = stiff[x] * fresh
                if x == 0:
                    head_x[k] = moved
                if x == size_x - 1:
                    tail_x[k] = moved
                head_y[k, x : x + 1] = moved[:1]
                tail_y[k, x : x + 1] = moved[size_y - 1 :]


def sweep(last, field, load, inverse, stiff, coupling, halo):
    _, size_x, size_y, size_z = field.shape
    shapes = [field.shape]
    if not last:
        shapes += [(3, size_y, size_z)] * 2 + [(3, size_x, size_z)] * 2

    def kernel(*refs):
        sweep_kernel(last, *refs)

    return pl.pallas_call(
        kernel,
        out_shape=[jax.ShapeDtypeStruct(shape, jnp.float32) for shape in shapes],
        scratch_shapes=[pltpu.VMEM((3, size_x + 2, size_y, size_z), jnp.float32)],
        compiler_params=pltpu.CompilerParams(vmem_limit_bytes=24 * MIB),
        name="sweep_cells",
    )(field, load, inverse, stiff, coupling, *halo)


def exchange(head_x, tail_x, head_y, tail_y):
    def shifted(face, axis, up):
        pairs = [(i, i + 1) if up else (i + 1, i) for i in range(lax.axis_size(axis) - 1)]
        return lax.ppermute(face, axis, pairs)

    return (
        shifted(tail_x, "gx", True),
        shifted(head_x, "gx", False),
        shifted(tail_y, "gy", True),
        shifted(head_y, "gy", False),
    )


def gather_kernel(ends, field, cells, weights, boxes, sums, hot, left, right, total):
    height, depth = field.shape[1:]
    lines, width = cells.shape
    half = depth // 2
    group = STEP_ROWS // width
    step = STEP_ROWS
    total[...] = jnp.zeros_like(total)
    right[...] = jnp.zeros_like(right)

    def chunk(i, _):
        rows = [pl.ds(i * group + q, 1) for q in range(group)]
        there = jnp.concatenate(
            [places(half, width) == (cells[row, :] & (half - 1)) for row in rows], axis=1
        )
        start, count = windows(ends, i)

        def window(w, picked):
            least = start + w * WINDOW
            base = pl.multiple_of(jnp.minimum(least, height - WINDOW), 8)
            for q in range(group):
                place = window_place(cells[rows[q], :], least, base)
                ones = marked(places(2 * WINDOW, width) == place, 1.0)
                hot[: 2 * WINDOW, q * width : (q + 1) * width] = ones
                hot[2 * WINDOW :, q * width : (q + 1) * width] = ones
            fresh = []
            for k in range(3):
                block = field[k, pl.ds(base, WINDOW), :]
                block = jnp.concatenate([block[:, :half], block[:, half:]], axis=0)
                high, low = halves(block)
                both = jnp.concatenate([high, low], axis=0).T.astype(jnp.bfloat16)
                part = jnp.dot(both, hot[...], preferred_element_type=jnp.float32)
                fresh.append(
                    picked[k] + jnp.sum(jnp.where(there, part, 0.0), axis=0, keepdims=True)
                )
            return tuple(fresh)

        picked = lax.fori_loop(
            0, count, window, tuple(jnp.zeros((1, step), jnp.float32) for k in range(3))
        )
        for q in range(group):
            at = slice(q * width, (q + 1) * width)
            low_at = slice(step + q * width, step + (q + 1) * width)
            weight = weights[rows[q], :]
            box = boxes[rows[q], :].astype(jnp.int32)
            owned = marked(places(left.shape[0], width) == box // BOX_DEV, 1.0)
            left[:, at] = owned
            left[:, low_at] = owned
            inside = places(BOX_DEV, width) == box % BOX_DEV
            for k in range(3):
                high, low = halves(picked[k][:, at] * weight)
                band = slice(k * BOX_DEV, (k + 1) * BOX_DEV)
                right[band, at] = marked(inside, high)
                right[band, low_at] = marked(inside, low)
        total[...] += dot_last(left[...], right[...])
        return 0

    lax.fori_loop(0, lines // group, chunk, 0)
    for p in range(2):
        sums[:, p, :] = total[:, p * 128 : (p + 1) * 128]


def gather(ends, field, cells, weights, boxes, devices):
    vmem = pl.BlockSpec(memory_space=pltpu.VMEM)
    return pl.pallas_call(
        gather_kernel,
        in_specs=[pl.BlockSpec(memory_space=pltpu.SMEM)] + [vmem] * 4,
        out_specs=vmem,
        out_shape=jax.ShapeDtypeStruct((devices, 2, 128), jnp.float32),
        scratch_shapes=[
            pltpu.VMEM((4 * WINDOW, STEP_ROWS), jnp.bfloat16),
            pltpu.VMEM((devices, 2 * STEP_ROWS), jnp.bfloat16),
            pltpu.VMEM((4 * BOX_DEV, 2 * STEP_ROWS), jnp.bfloat16),
            pltpu.VMEM((devices, 4 * BOX_DEV), jnp.float32),
        ],
        compiler_params=pltpu.CompilerParams(vmem_limit_bytes=16 * MIB),
        name="gather_rows",
    )(ends, field, cells, weights, boxes)


def swapped(blocks):
    return lax.all_to_all(blocks, AXES, split_axis=0, concat_axis=0, tiled=True)


def body(
    sensitivity,
    node_weight,
    dest_device,
    dest_cell,
    box_owner,
    box_slot,
    stiffness,
    anchor,
    coupling,
):
    devices = lax.axis_size("gx") * lax.axis_size("gy")
    count = sensitivity.shape[1]
    size_x, size_y, size_z = stiffness.shape
    lane = lambda values: values.reshape(1, count)
    rows = pack(
        sensitivity,
        lane(node_weight),
        lane(dest_device),
        lane(dest_cell),
        lane(box_owner),
        lane(box_slot),
        devices,
    )
    rows = swapped(rows)
    planes = [rows[:, p].reshape(-1) for p in range(6)]
    keys = jnp.maximum(planes[3].astype(jnp.int32) - CELL_SHIFT, -1)
    ordered = lax.sort((keys, *planes[:3], *planes[4:]), num_keys=1, is_stable=False)
    cells, *values, weights, boxes = [part.reshape(-1, 128) for part in ordered]
    blocks = cells.reshape(-1, STEP_ROWS // 128, 128)
    ends = jnp.stack([blocks[:, 0, 0], blocks[:, -1, -1]])
    diagonal = 6.0 * stiffness[None] + anchor + jnp.stack([coupling[0], coupling[4], coupling[8]])
    inverse = 1.0 / diagonal
    load = scatter(ends, cells, values, size_x * size_y, size_z).reshape(3, size_x, size_y, size_z)
    field = load * inverse
    moved = stiffness[None] * field
    faces = (moved[:, 0], moved[:, -1], moved[:, :, 0], moved[:, :, -1])
    for turn in range(1, SWEEPS):
        last = turn == SWEEPS - 1
        field, *faces = sweep(
            last, field, load, inverse, stiffness, coupling, exchange(*faces)
        )
    flat = field.reshape(3, size_x * size_y, size_z)
    partial = gather(ends, flat, cells, weights, boxes, devices)
    summed = jnp.sum(swapped(partial), axis=0).reshape(4, BOX_DEV)
    return (field, summed[:3])


def solution(mesh):
    placed = (
        P(None, AXES),
        P(AXES),
        P(AXES, None),
        P(AXES),
        P(AXES, None),
        P(AXES),
        P("gx", "gy", None),
        P(None, "gx", "gy", None),
        P(None, "gx", "gy", None),
    )
    return jax.shard_map(
        body,
        mesh=mesh,
        in_specs=placed,
        out_specs=(P(None, "gx", "gy", None), P(None, AXES)),
        check_vma=False,
    )
```

```python
import jax
import jax.numpy as jnp
from jax import lax
from jax.experimental import pallas as pl
from jax.experimental.pallas import tpu as pltpu
from jax.sharding import PartitionSpec as P

BOX_DEV = 64
BOX_BITS = 6
SWEEPS = 4
AXES = ("gx", "gy")
STEP_ROWS = 512
RANK_ROWS = 256
WINDOW = 32
SIDE = 4
CELL_SHIFT = 257
MIB = 1024 * 1024


def dot_last(left, right):
    return lax.dot_general(
        left, right, (((1,), (1,)), ((), ())), preferred_element_type=jnp.float32
    )


def halves(values):
    high = values.astype(jnp.bfloat16).astype(jnp.float32)
    return high, values - high


def places(height, width):
    return lax.broadcasted_iota(jnp.int32, (height, width), 0)


def marked(mask, row):
    return jnp.where(mask, row, 0.0).astype(jnp.bfloat16)


def pack_kernel(*refs):
    given, rows, kept = refs[:6], refs[6], refs[7:13]
    ranks, upper, left, right, total, arrivals = refs[13:]
    sens, weight, device, cell, owner, slot = kept
    devices, _, capacity = rows.shape
    part = upper.shape[0]
    step = STEP_ROWS
    steps = sens.shape[1] // step
    copies = [
        pltpu.make_async_copy(given[p], kept[p], arrivals.at[p]) for p in range(len(given))
    ]
    for copy in copies:
        copy.start()
    before = lax.broadcasted_iota(jnp.int32, (part, part), 0)
    after = lax.broadcasted_iota(jnp.int32, (part, part), 1)
    upper[...] = marked(before < after, 1.0)
    total[...] = jnp.zeros_like(total)
    for copy in copies:
        copy.wait()

    def rank(i, base):
        for b in range(4):
            at = pl.ds(pl.multiple_of((i * 4 + b) * part, part), part)
            here = places(devices, part) == device[:, at]
            ones = jnp.where(here, 1.0, 0.0)
            within = jnp.dot(
                ones.astype(jnp.bfloat16), upper[...], preferred_element_type=jnp.float32
            )
            ranks[:, at] = jnp.sum(
                jnp.where(here, within + base, 0.0), axis=0, keepdims=True
            ).astype(jnp.int32)
            base = base + jnp.sum(ones, axis=1, keepdims=True)
        return base

    lax.fori_loop(0, sens.shape[1] // part // 4, rank, jnp.zeros((devices, 1), jnp.float32))

    def chunk(i, _):
        for b in range(2):
            at = pl.ds(pl.multiple_of((i * 2 + b) * step, step), step)
            ones = marked(places(devices, step) == device[:, at], 1.0)
            left[b, :, :step] = ones
            left[b, :, step:] = ones
            here = places(capacity, step) == ranks[:, at]
            own_cell = cell[:, at]
            pairs = [halves(sens[k : k + 1, at]) for k in range(3)]
            pairs.append(
                (
                    (((own_cell >> 9) + 1) << 9).astype(jnp.float32),
                    ((own_cell & 511) + (CELL_SHIFT - 512)).astype(jnp.float32),
                )
            )
            pairs.append(halves(weight[:, at]))
            pairs.append(
                ((owner[:, at] * BOX_DEV).astype(jnp.float32), slot[:, at].astype(jnp.float32))
            )
            for p, (high, low) in enumerate(pairs):
                band = slice(p * capacity, (p + 1) * capacity)
                right[b, band, :step] = marked(here, high)
                right[b, band, step:] = marked(here, low)
        total[...] += dot_last(left[0], right[0]) + dot_last(left[1], right[1])
        return 0

    lax.fori_loop(0, steps // 2, chunk, 0)
    for p in range(6):
        rows[:, p, :] = total[:, p * capacity : (p + 1) * capacity]
    for p in range(6, 8):
        rows[:, p, :] = jnp.zeros((devices, capacity), jnp.float32)


def pack(devices, *given):
    count = given[0].shape[1]
    capacity = 2 * count // devices
    return pl.pallas_call(
        pack_kernel,
        in_specs=[pl.BlockSpec(memory_space=pltpu.HBM)] * len(given),
        out_shape=jax.ShapeDtypeStruct((devices, 8, capacity), jnp.float32),
        scratch_shapes=[pltpu.VMEM(part.shape, part.dtype) for part in given]
        + [
            pltpu.VMEM((1, count), jnp.int32),
            pltpu.VMEM((RANK_ROWS, RANK_ROWS), jnp.bfloat16),
            pltpu.VMEM((2, devices, 2 * STEP_ROWS), jnp.bfloat16),
            pltpu.VMEM((2, 6 * capacity, 2 * STEP_ROWS), jnp.bfloat16),
            pltpu.VMEM((devices, 6 * capacity), jnp.float32),
            pltpu.SemaphoreType.DMA((len(given),)),
        ],
        compiler_params=pltpu.CompilerParams(vmem_limit_bytes=20 * MIB),
        name="pack_rows",
    )(*given)


def windows(ends, i):
    first = jnp.maximum(ends[0, i] >> 8, 0)
    start = first & ~7
    return start, (jnp.maximum((ends[1, i] >> 8) + WINDOW - start, 0)) // WINDOW


def filled(ends):
    groups = ends.shape[1] // SIDE

    def count(g, empty):
        return empty + jnp.where(ends[1, g * SIDE + SIDE - 1] < 0, 1, 0)

    return lax.fori_loop(0, groups, count, 0)


def scatter_kernel(ends, cells, one, two, three, inverse, stiff, load, field, *rest):
    head_x, tail_x, head_y, tail_y, left, right = rest
    height, depth = load.shape[1:]
    lines, width = cells.shape
    half = depth // 2
    group = STEP_ROWS // width
    step = STEP_ROWS
    load[...] = jnp.zeros_like(load)

    def fill(i, b):
        for q in range(group):
            row = pl.ds(i * group + q, 1)
            there = places(half, width) == (cells[row, :] & (half - 1))
            for k, sens in enumerate((one, two, three)):
                high, low = halves(sens[row, :])
                band = slice(k * half, (k + 1) * half)
                right[b, band, q * width : (q + 1) * width] = marked(there, high)
                right[b, band, step + q * width : step + (q + 1) * width] = marked(there, low)

    def window(i, b, start, w):
        least = start + w * WINDOW
        base = pl.multiple_of(jnp.minimum(least, height - WINDOW), 8)
        for q in range(group):
            cell = cells[pl.ds(i * group + q, 1), :]
            hot = marked(places(2 * WINDOW, width) == window_place(cell, least, base), 1.0)
            left[b, :, q * width : (q + 1) * width] = hot
            left[b, :, step + q * width : step + (q + 1) * width] = hot
        sums = dot_last(left[b], right[b])

        def add():
            for k in range(3):
                for side in range(2):
                    at = (k, pl.ds(base, WINDOW), slice(side * half, (side + 1) * half))
                    load[at] += sums[
                        side * WINDOW : (side + 1) * WINDOW, k * half : (k + 1) * half
                    ]

        return add

    def chunks(i, _):
        own = [i * SIDE + b for b in range(SIDE)]
        spans = [windows(ends, j) for j in own]
        for b in range(SIDE):
            fill(own[b], b)
        adds = [window(own[b], b, spans[b][0], 0) for b in range(SIDE)]
        for add in adds:
            add()
        for b in range(SIDE):

            def more(w, _, b=b):
                window(own[b], b, spans[b][0], w)()
                return 0

            lax.fori_loop(1, spans[b][1], more, 0)
        return 0

    lax.fori_loop(filled(ends), lines // group // SIDE, chunks, 0)
    size_x, size_y = head_y.shape[1], head_x.shape[1]
    for k in range(3):
        field[k] = load[k] * inverse[k]
        head_x[k] = field[k, :size_y] * stiff[:size_y]
        tail_x[k] = field[k, height - size_y :] * stiff[height - size_y :]
        for x in range(size_x):
            for y, face in ((0, head_y), (size_y - 1, tail_y)):
                at = slice(x * size_y + y, x * size_y + y + 1)
                face[k, x : x + 1] = field[k, at] * stiff[at]


def window_place(cell, least, base):
    line = cell >> 8
    place = ((cell >> 7) & 1) * WINDOW + line - base
    inside = (line >= least) & (line < base + WINDOW)
    return jnp.where(inside, place, -1)


def scatter(ends, cells, values, inverse, stiff):
    size_x, size_y, depth = stiff.shape
    height = size_x * size_y
    vmem = pl.BlockSpec(memory_space=pltpu.VMEM)
    cube = (3, height, depth)
    shapes = [cube] * 2 + [(3, size_y, depth)] * 2 + [(3, size_x, depth)] * 2
    load, field, *faces = pl.pallas_call(
        scatter_kernel,
        in_specs=[pl.BlockSpec(memory_space=pltpu.SMEM)] + [vmem] * 6,
        out_specs=[vmem] * 6,
        out_shape=[jax.ShapeDtypeStruct(shape, jnp.float32) for shape in shapes],
        scratch_shapes=[
            pltpu.VMEM((SIDE, 2 * WINDOW, 2 * STEP_ROWS), jnp.bfloat16),
            pltpu.VMEM((SIDE, 3 * depth // 2, 2 * STEP_ROWS), jnp.bfloat16),
        ],
        compiler_params=pltpu.CompilerParams(vmem_limit_bytes=20 * MIB),
        name="scatter_rows",
    )(ends, cells, *values, inverse.reshape(cube), stiff.reshape(cube[1:]))
    whole = (3, size_x, size_y, depth)
    return load.reshape(whole), field.reshape(whole), faces


def sweep_kernel(last, field, load, inverse, stiff, coupling, west, east, south, north, *outs):
    _, size_x, size_y, size_z = field.shape
    padded = outs[-1]
    result = outs[0]
    padded[:, 0] = west[...]
    padded[:, size_x + 1] = east[...]
    for x in range(size_x):
        for k in range(3):
            padded[k, x + 1] = stiff[x] * field[k, x]
    row = lax.broadcasted_iota(jnp.int32, (size_y, size_z), 0)
    column = lax.broadcasted_iota(jnp.int32, (size_y, size_z), 1)
    for x in range(size_x):
        own = [field[k, x] for k in range(3)]
        for k in range(3):
            middle = padded[k, x + 1]
            total = load[k, x] + padded[k, x] + padded[k, x + 2]
            total = total + jnp.where(row == 0, south[k, x : x + 1], pltpu.roll(middle, 1, 0))
            total = total + jnp.where(
                row == size_y - 1, north[k, x : x + 1], pltpu.roll(middle, size_y - 1, 0)
            )
            total = total + jnp.where(column == 0, 0.0, pltpu.roll(middle, 1, 1))
            total = total + jnp.where(
                column == size_z - 1, 0.0, pltpu.roll(middle, size_z - 1, 1)
            )
            for j in range(3):
                if j != k:
                    total = total - coupling[3 * j + k, x] * own[j]
            fresh = total * inverse[k, x]
            result[k, x] = fresh
            if not last:
                head_x, tail_x, head_y, tail_y = outs[1:5]
                moved = stiff[x] * fresh
                if x == 0:
                    head_x[k] = moved
                if x == size_x - 1:
                    tail_x[k] = moved
                head_y[k, x : x + 1] = moved[:1]
                tail_y[k, x : x + 1] = moved[size_y - 1 :]


def sweep(last, field, load, inverse, stiff, coupling, halo):
    _, size_x, size_y, size_z = field.shape
    shapes = [field.shape]
    if not last:
        shapes += [(3, size_y, size_z)] * 2 + [(3, size_x, size_z)] * 2

    def kernel(*refs):
        sweep_kernel(last, *refs)

    return pl.pallas_call(
        kernel,
        out_shape=[jax.ShapeDtypeStruct(shape, jnp.float32) for shape in shapes],
        scratch_shapes=[pltpu.VMEM((3, size_x + 2, size_y, size_z), jnp.float32)],
        compiler_params=pltpu.CompilerParams(vmem_limit_bytes=24 * MIB),
        name="sweep_cells",
    )(field, load, inverse, stiff, coupling, *halo)


def exchange(head_x, tail_x, head_y, tail_y):
    def shifted(face, axis, up):
        pairs = [(i, i + 1) if up else (i + 1, i) for i in range(lax.axis_size(axis) - 1)]
        return lax.ppermute(face, axis, pairs)

    south = shifted(tail_y, "gy", True)
    north = shifted(head_y, "gy", False)
    west = shifted(tail_x, "gx", True)
    east = shifted(head_x, "gx", False)
    return west, east, south, north


def gather_kernel(ends, field, cells, weights, boxes, sums, hot, left, right, total):
    height, depth = field.shape[1:]
    lines, width = cells.shape
    half = depth // 2
    group = STEP_ROWS // width
    step = STEP_ROWS
    total[...] = jnp.zeros_like(total)
    right[...] = jnp.zeros_like(right)

    def rows(i):
        return [pl.ds(i * group + q, 1) for q in range(group)]

    def window(i, b, start, w):
        least = start + w * WINDOW
        base = pl.multiple_of(jnp.minimum(least, height - WINDOW), 8)
        own = [cells[row, :] for row in rows(i)]
        for q in range(group):
            ones = marked(places(2 * WINDOW, width) == window_place(own[q], least, base), 1.0)
            hot[b, : 2 * WINDOW, q * width : (q + 1) * width] = ones
            hot[b, 2 * WINDOW :, q * width : (q + 1) * width] = ones
        there = [places(half, width) == (cell & (half - 1)) for cell in own]
        picked = []
        for k in range(3):
            block = field[k, pl.ds(base, WINDOW), :]
            block = jnp.concatenate([block[:, :half], block[:, half:]], axis=0)
            high, low = halves(block)
            both = jnp.concatenate([high, low], axis=0).T.astype(jnp.bfloat16)
            part = jnp.dot(both, hot[b], preferred_element_type=jnp.float32)
            picked.append(
                jnp.concatenate(
                    [
                        jnp.sum(
                            jnp.where(there[q], part[:, q * width : (q + 1) * width], 0.0),
                            axis=0,
                            keepdims=True,
                        )
                        for q in range(group)
                    ],
                    axis=1,
                )
            )
        return tuple(picked)

    def spread(i, b, picked):
        for q, row in enumerate(rows(i)):
            at = slice(q * width, (q + 1) * width)
            low_at = slice(step + q * width, step + (q + 1) * width)
            weight = weights[row, :]
            box = boxes[row, :].astype(jnp.int32)
            owned = marked(places(left.shape[1], width) == (box >> BOX_BITS), 1.0)
            left[b, :, at] = owned
            left[b, :, low_at] = owned
            inside = places(BOX_DEV, width) == (box & (BOX_DEV - 1))
            for k in range(3):
                high, low = halves(picked[k][:, at] * weight)
                band = slice(k * BOX_DEV, (k + 1) * BOX_DEV)
                right[b, band, at] = marked(inside, high)
                right[b, band, low_at] = marked(inside, low)

    def chunks(i, _):
        own = [i * SIDE + b for b in range(SIDE)]
        spans = [windows(ends, j) for j in own]
        firsts = [window(own[b], b, spans[b][0], 0) for b in range(SIDE)]
        finals = []
        for b in range(SIDE):

            def more(w, picked, b=b):
                fresh = window(own[b], b, spans[b][0], w)
                return tuple(old + new for old, new in zip(picked, fresh))

            finals.append(lax.fori_loop(1, spans[b][1], more, firsts[b]))
        for b in range(SIDE):
            spread(own[b], b, finals[b])
        parts = [dot_last(left[b], right[b]) for b in range(SIDE)]
        total[...] += sum(parts[1:], parts[0])
        return 0

    lax.fori_loop(filled(ends), lines // group // SIDE, chunks, 0)
    for p in range(2):
        sums[:, p, :] = total[:, p * 128 : (p + 1) * 128]


def gather(ends, field, cells, weights, boxes, devices):
    vmem = pl.BlockSpec(memory_space=pltpu.VMEM)
    return pl.pallas_call(
        gather_kernel,
        in_specs=[pl.BlockSpec(memory_space=pltpu.SMEM)] + [vmem] * 4,
        out_specs=vmem,
        out_shape=jax.ShapeDtypeStruct((devices, 2, 128), jnp.float32),
        scratch_shapes=[
            pltpu.VMEM((SIDE, 4 * WINDOW, STEP_ROWS), jnp.bfloat16),
            pltpu.VMEM((SIDE, devices, 2 * STEP_ROWS), jnp.bfloat16),
            pltpu.VMEM((SIDE, 4 * BOX_DEV, 2 * STEP_ROWS), jnp.bfloat16),
            pltpu.VMEM((devices, 4 * BOX_DEV), jnp.float32),
        ],
        compiler_params=pltpu.CompilerParams(vmem_limit_bytes=16 * MIB),
        name="gather_rows",
    )(ends, field, cells, weights, boxes)


def swapped(blocks):
    return lax.all_to_all(blocks, AXES, split_axis=0, concat_axis=0, tiled=True)


def body(
    sensitivity,
    node_weight,
    dest_device,
    dest_cell,
    box_owner,
    box_slot,
    stiffness,
    anchor,
    coupling,
):
    devices = lax.axis_size("gx") * lax.axis_size("gy")
    count = sensitivity.shape[1]
    size_x, size_y, size_z = stiffness.shape
    lane = lambda values: values.reshape(1, count)
    rows = pack(
        devices,
        sensitivity,
        lane(node_weight),
        lane(dest_device),
        lane(dest_cell),
        lane(box_owner),
        lane(box_slot),
    )
    rows = swapped(rows)
    planes = [rows[:, p].reshape(-1) for p in range(6)]
    keys = jnp.maximum(planes[3].astype(jnp.int32) - CELL_SHIFT, -1)
    ordered = lax.sort((keys, *planes[:3], *planes[4:]), num_keys=1, is_stable=False)
    cells, *values, weights, boxes = [part.reshape(-1, 128) for part in ordered]
    blocks = cells.reshape(-1, STEP_ROWS // 128, 128)
    ends = jnp.stack([blocks[:, 0, 0], blocks[:, -1, -1]])
    diagonal = 6.0 * stiffness[None] + anchor + jnp.stack([coupling[0], coupling[4], coupling[8]])
    inverse = 1.0 / diagonal
    load, field, faces = scatter(ends, cells, values, inverse, stiffness)
    for turn in range(1, SWEEPS):
        last = turn == SWEEPS - 1
        field, *faces = sweep(
            last, field, load, inverse, stiffness, coupling, exchange(*faces)
        )
    flat = field.reshape(3, size_x * size_y, size_z)
    partial = gather(ends, flat, cells, weights, boxes, devices)
    summed = jnp.sum(swapped(partial), axis=0).reshape(4, BOX_DEV)
    return (field, summed[:3])


def solution(mesh):
    placed = (
        P(None, AXES),
        P(AXES),
        P(AXES, None),
        P(AXES),
        P(AXES, None),
        P(AXES),
        P("gx", "gy", None),
        P(None, "gx", "gy", None),
        P(None, "gx", "gy", None),
    )
    return jax.shard_map(
        body,
        mesh=mesh,
        in_specs=placed,
        out_specs=(P(None, "gx", "gy", None), P(None, AXES)),
        check_vma=False,
    )
```

```python
import jax
import jax.numpy as jnp
from jax import lax
from jax.experimental import pallas as pl
from jax.experimental.pallas import tpu as pltpu
from jax.sharding import PartitionSpec as P

BOX_DEV = 64
BOX_BITS = 6
SWEEPS = 4
AXES = ("gx", "gy")
STEP_ROWS = 512
RANK_ROWS = 256
WINDOW = 32
SIDE = 8
PARTS = 4
CELL_SHIFT = 257
MIB = 1024 * 1024


def dot_last(left, right):
    return lax.dot_general(
        left, right, (((1,), (1,)), ((), ())), preferred_element_type=jnp.float32
    )


def halves(values):
    high = values.astype(jnp.bfloat16).astype(jnp.float32)
    return high, values - high


def places(height, width):
    return lax.broadcasted_iota(jnp.int32, (height, width), 0)


def marked(mask, row):
    return jnp.where(mask, row, 0.0).astype(jnp.bfloat16)


def pack_kernel(*refs):
    given, rows, kept = refs[:6], refs[6], refs[7:13]
    ranks, upper, left, right, total, arrivals = refs[13:]
    sens, weight, device, cell, owner, slot = kept
    devices, _, capacity = rows.shape
    half = capacity // 2
    part = upper.shape[0]
    step = STEP_ROWS
    steps = sens.shape[1] // step
    copies = [
        pltpu.make_async_copy(given[p], kept[p], arrivals.at[p]) for p in range(len(given))
    ]
    for copy in copies:
        copy.start()
    before = lax.broadcasted_iota(jnp.int32, (part, part), 0)
    after = lax.broadcasted_iota(jnp.int32, (part, part), 1)
    upper[...] = marked(before < after, 1.0)
    total[...] = jnp.zeros_like(total)
    for copy in copies:
        copy.wait()

    def rank(i, base):
        for b in range(4):
            at = pl.ds(pl.multiple_of((i * 4 + b) * part, part), part)
            here = places(devices, part) == device[:, at]
            ones = jnp.where(here, 1.0, 0.0)
            within = jnp.dot(
                ones.astype(jnp.bfloat16), upper[...], preferred_element_type=jnp.float32
            )
            ranks[:, at] = jnp.sum(
                jnp.where(here, within + base, 0.0), axis=0, keepdims=True
            ).astype(jnp.int32)
            base = base + jnp.sum(ones, axis=1, keepdims=True)
        return base

    lax.fori_loop(0, sens.shape[1] // part // 4, rank, jnp.zeros((devices, 1), jnp.float32))

    def chunk(i, _):
        for b in range(2):
            at = pl.ds(pl.multiple_of((i * 2 + b) * step, step), step)
            rank = ranks[:, at]
            lane = device[:, at] + jnp.where(rank >= half, devices, 0)
            ones = marked(places(2 * devices, step) == lane, 1.0)
            left[b, :, :step] = ones
            left[b, :, step:] = ones
            here = places(half, step) == (rank & (half - 1))
            own_cell = cell[:, at]
            pairs = [halves(sens[k : k + 1, at]) for k in range(3)]
            pairs.append(
                (
                    (((own_cell >> 9) + 1) << 9).astype(jnp.float32),
                    ((own_cell & 511) + (CELL_SHIFT - 512)).astype(jnp.float32),
                )
            )
            pairs.append(halves(weight[:, at]))
            pairs.append(
                ((owner[:, at] * BOX_DEV).astype(jnp.float32), slot[:, at].astype(jnp.float32))
            )
            for p, (high, low) in enumerate(pairs):
                band = slice(p * half, (p + 1) * half)
                right[b, band, :step] = marked(here, high)
                right[b, band, step:] = marked(here, low)
        total[...] += dot_last(right[0], left[0]) + dot_last(right[1], left[1])
        return 0

    lax.fori_loop(0, steps // 2, chunk, 0)
    for p in range(6):
        band = total[p * half : (p + 1) * half, :]
        rows[:, p, :] = jnp.concatenate([band[:, :devices].T, band[:, devices:].T], axis=1)
    for p in range(6, 8):
        rows[:, p, :] = jnp.zeros((devices, capacity), jnp.float32)


def pack(devices, *given):
    count = given[0].shape[1]
    capacity = 2 * count // devices
    return pl.pallas_call(
        pack_kernel,
        in_specs=[pl.BlockSpec(memory_space=pltpu.HBM)] * len(given),
        out_shape=jax.ShapeDtypeStruct((devices, 8, capacity), jnp.float32),
        scratch_shapes=[pltpu.VMEM(part.shape, part.dtype) for part in given]
        + [
            pltpu.VMEM((1, count), jnp.int32),
            pltpu.VMEM((RANK_ROWS, RANK_ROWS), jnp.bfloat16),
            pltpu.VMEM((2, 2 * devices, 2 * STEP_ROWS), jnp.bfloat16),
            pltpu.VMEM((2, 3 * capacity, 2 * STEP_ROWS), jnp.bfloat16),
            pltpu.VMEM((3 * capacity, 2 * devices), jnp.float32),
            pltpu.SemaphoreType.DMA((len(given),)),
        ],
        compiler_params=pltpu.CompilerParams(vmem_limit_bytes=58 * MIB),
        name="pack_rows",
    )(*given)


def windows(ends, i):
    first = jnp.maximum(ends[0, i] >> 8, 0)
    start = first & ~7
    return start, (jnp.maximum((ends[1, i] >> 8) + WINDOW - start, 0)) // WINDOW


def filled(ends):
    groups = ends.shape[1] // SIDE

    def count(g, empty):
        return empty + jnp.where(ends[1, g * SIDE + SIDE - 1] < 0, 1, 0)

    return lax.fori_loop(0, groups, count, 0)


def scatter_kernel(*refs):
    ends, cells, one, two, three, stiff_at, anchor_at, coupling_at = refs[:8]
    load, scaled, inverse, stiff, head_x, tail_x, head_y, tail_y = refs[8:16]
    anchor, coupling, left, right, arrivals = refs[16:]
    copies = [
        pltpu.make_async_copy(source, target, arrivals.at[p])
        for p, (source, target) in enumerate(
            ((stiff_at, stiff), (anchor_at, anchor), (coupling_at, coupling))
        )
    ]
    for copy in copies:
        copy.start()
    height, depth = load.shape[1:]
    lines, width = cells.shape
    part = depth // PARTS
    group = STEP_ROWS // width
    step = STEP_ROWS
    load[...] = jnp.zeros_like(load)

    def fill(i, b):
        for q in range(group):
            row = pl.ds(i * group + q, 1)
            there = places(part, width) == (cells[row, :] & (part - 1))
            for k, sens in enumerate((one, two, three)):
                high, low = halves(sens[row, :])
                band = slice(k * part, (k + 1) * part)
                right[b, band, q * width : (q + 1) * width] = marked(there, high)
                right[b, band, step + q * width : step + (q + 1) * width] = marked(there, low)

    def window(i, b, start, w):
        least = start + w * WINDOW
        base = pl.multiple_of(jnp.minimum(least, height - WINDOW), 8)
        for q in range(group):
            cell = cells[pl.ds(i * group + q, 1), :]
            place = window_place(cell, least, base, PARTS)
            hot = marked(places(PARTS * WINDOW, width) == place, 1.0)
            left[b, :, q * width : (q + 1) * width] = hot
            left[b, :, step + q * width : step + (q + 1) * width] = hot
        sums = dot_last(left[b], right[b])

        def add():
            for k in range(3):
                for side in range(PARTS // 2):
                    at = (k, pl.ds(base, WINDOW), slice(side * 2 * part, (side + 1) * 2 * part))
                    load[at] += jnp.concatenate(
                        [
                            sums[p * WINDOW : (p + 1) * WINDOW, k * part : (k + 1) * part]
                            for p in (2 * side, 2 * side + 1)
                        ],
                        axis=1,
                    )

        return add

    def chunks(i, _):
        own = [i * SIDE + b for b in range(SIDE)]
        spans = [windows(ends, j) for j in own]
        for b in range(SIDE):
            fill(own[b], b)
        adds = [window(own[b], b, spans[b][0], 0) for b in range(SIDE)]
        for add in adds:
            add()
        for b in range(SIDE):

            def more(w, _, b=b):
                window(own[b], b, spans[b][0], w)()
                return 0

            lax.fori_loop(1, spans[b][1], more, 0)
        return 0

    lax.fori_loop(filled(ends), lines // group // SIDE, chunks, 0)
    for copy in copies:
        copy.wait()
    size_x, size_y = head_y.shape[1], head_x.shape[1]
    for x in range(size_x):
        at = slice(x * size_y, (x + 1) * size_y)
        weight = stiff[at]
        for k in range(3):
            own = 1.0 / (6.0 * weight + anchor[k, at] + coupling[4 * k, at])
            inverse[k, at] = own
            for place, j in enumerate(others(k)):
                scaled[2 * k + place, at] = coupling[3 * j + k, at] * own
            fresh = load[k, at] * own
            load[k, at] = fresh
            moved = weight * fresh
            if x == 0:
                head_x[k] = moved
            if x == size_x - 1:
                tail_x[k] = moved
            head_y[k, x : x + 1] = moved[:1]
            tail_y[k, x : x + 1] = moved[size_y - 1 :]


def window_place(cell, least, base, parts):
    line = cell >> 8
    place = ((cell & 255) * parts >> 8) * WINDOW + line - base
    inside = (line >= least) & (line < base + WINDOW)
    return jnp.where(inside, place, -1)


def scatter(ends, cells, values, stiff, anchor, coupling):
    size_x, size_y, depth = stiff.shape
    height = size_x * size_y
    vmem = pl.BlockSpec(memory_space=pltpu.VMEM)
    shapes = [(3, height, depth), (6, height, depth), (3, height, depth), (height, depth)]
    shapes += [(3, size_y, depth)] * 2 + [(3, size_x, depth)] * 2
    outs = pl.pallas_call(
        scatter_kernel,
        in_specs=[pl.BlockSpec(memory_space=pltpu.SMEM)]
        + [vmem] * 4
        + [pl.BlockSpec(memory_space=pltpu.HBM)] * 3,
        out_specs=[vmem] * 8,
        out_shape=[jax.ShapeDtypeStruct(shape, jnp.float32) for shape in shapes],
        scratch_shapes=[
            pltpu.VMEM((3, height, depth), jnp.float32),
            pltpu.VMEM((9, height, depth), jnp.float32),
            pltpu.VMEM((SIDE, PARTS * WINDOW, 2 * STEP_ROWS), jnp.bfloat16),
            pltpu.VMEM((SIDE, 3 * depth // PARTS, 2 * STEP_ROWS), jnp.bfloat16),
            pltpu.SemaphoreType.DMA((3,)),
        ],
        compiler_params=pltpu.CompilerParams(vmem_limit_bytes=24 * MIB),
        name="scatter_rows",
    )(
        ends,
        cells,
        *values,
        *(part.reshape(*part.shape[:-3], height, depth) for part in (stiff, anchor, coupling)),
    )
    cells_of = [part.reshape(*part.shape[:-2], size_x, size_y, depth) for part in outs[:4]]
    return cells_of, outs[4:]


def swept(first, scaled, inverse, stiff, field, halo, padded, store):
    _, size_x, size_y, size_z = field.shape
    south, north, west, east = halo
    padded[:, 0] = west[...]
    padded[:, size_x + 1] = east[...]
    for x in range(size_x):
        for k in range(3):
            padded[k, x + 1] = stiff[x] * field[k, x]
    row = lax.broadcasted_iota(jnp.int32, (size_y, size_z), 0)
    column = lax.broadcasted_iota(jnp.int32, (size_y, size_z), 1)
    for x in range(size_x):
        own = [field[k, x] for k in range(3)]
        for k in range(3):
            middle = padded[k, x + 1]
            total = padded[k, x] + padded[k, x + 2]
            total = total + jnp.where(row == 0, south[k, x : x + 1], pltpu.roll(middle, 1, 0))
            total = total + jnp.where(
                row == size_y - 1, north[k, x : x + 1], pltpu.roll(middle, size_y - 1, 0)
            )
            total = total + jnp.where(column == 0, 0.0, pltpu.roll(middle, 1, 1))
            total = total + jnp.where(
                column == size_z - 1, 0.0, pltpu.roll(middle, size_z - 1, 1)
            )
            fresh = first[k, x] + total * inverse[k, x]
            for place, j in enumerate(others(k)):
                fresh = fresh - scaled[2 * k + place, x] * own[j]
            store(k, x, fresh)


def others(k):
    return [j for j in range(3) if j != k]


def sweep_kernel(first, scaled, inverse, stiff, field, south, north, west, east, *outs):
    result, head_x, tail_x, head_y, tail_y, padded = outs
    size_x, size_y = field.shape[1:3]

    def store(k, x, fresh):
        result[k, x] = fresh
        moved = stiff[x] * fresh
        if x == 0:
            head_x[k] = moved
        if x == size_x - 1:
            tail_x[k] = moved
        head_y[k, x : x + 1] = moved[:1]
        tail_y[k, x : x + 1] = moved[size_y - 1 :]

    swept(first, scaled, inverse, stiff, field, (south, north, west, east), padded, store)


def sweep(*given):
    _, size_x, size_y, size_z = given[0].shape
    shapes = [given[0].shape] + [(3, size_y, size_z)] * 2 + [(3, size_x, size_z)] * 2
    return pl.pallas_call(
        sweep_kernel,
        out_shape=[jax.ShapeDtypeStruct(shape, jnp.float32) for shape in shapes],
        scratch_shapes=[pltpu.VMEM((3, size_x + 2, size_y, size_z), jnp.float32)],
        compiler_params=pltpu.CompilerParams(vmem_limit_bytes=8 * MIB),
        name="sweep_cells",
    )(*given)


def exchange(head_x, tail_x, head_y, tail_y):
    def shifted(face, axis, up):
        pairs = [(i, i + 1) if up else (i + 1, i) for i in range(lax.axis_size(axis) - 1)]
        return lax.ppermute(face, axis, pairs)

    south = shifted(tail_y, "gy", True)
    north = shifted(head_y, "gy", False)
    west = shifted(tail_x, "gx", True)
    east = shifted(head_x, "gx", False)
    return south, north, west, east


def gather_kernel(*refs):
    ends, first, scaled, inverse, stiff, before, south, north, west, east = refs[:10]
    cells, weights, boxes, final, sums, padded, field, hot, left, right, total, sent = refs[10:]
    size_y = before.shape[2]

    def store(k, x, fresh):
        field[k, x * size_y : (x + 1) * size_y] = fresh

    swept(first, scaled, inverse, stiff, before, (south, north, west, east), padded, store)
    out = pltpu.make_async_copy(field, final, sent)
    out.start()
    height, depth = field.shape[1:]
    lines, width = cells.shape
    half = depth // 2
    group = STEP_ROWS // width
    step = STEP_ROWS
    total[...] = jnp.zeros_like(total)
    right[...] = jnp.zeros_like(right)

    def rows(i):
        return [pl.ds(i * group + q, 1) for q in range(group)]

    def window(i, b, start, w):
        least = start + w * WINDOW
        base = pl.multiple_of(jnp.minimum(least, height - WINDOW), 8)
        own = [cells[row, :] for row in rows(i)]
        for q in range(group):
            ones = marked(places(2 * WINDOW, width) == window_place(own[q], least, base, 2), 1.0)
            hot[b, : 2 * WINDOW, q * width : (q + 1) * width] = ones
            hot[b, 2 * WINDOW :, q * width : (q + 1) * width] = ones
        there = [places(half, width) == (cell & (half - 1)) for cell in own]
        picked = []
        block = jnp.concatenate(
            [
                jnp.concatenate(
                    [field[k, pl.ds(base, WINDOW), side * half : (side + 1) * half] for k in range(3)],
                    axis=1,
                )
                for side in range(2)
            ],
            axis=0,
        )
        both = jnp.concatenate(halves(block), axis=0).T.astype(jnp.bfloat16)
        parts = jnp.dot(both, hot[b], preferred_element_type=jnp.float32)
        for k in range(3):
            part = parts[k * half : (k + 1) * half]
            picked.append(
                jnp.concatenate(
                    [
                        jnp.sum(
                            jnp.where(there[q], part[:, q * width : (q + 1) * width], 0.0),
                            axis=0,
                            keepdims=True,
                        )
                        for q in range(group)
                    ],
                    axis=1,
                )
            )
        return tuple(picked)

    def spread(i, b, picked):
        for q, row in enumerate(rows(i)):
            at = slice(q * width, (q + 1) * width)
            low_at = slice(step + q * width, step + (q + 1) * width)
            weight = weights[row, :]
            box = boxes[row, :].astype(jnp.int32)
            owned = marked(places(left.shape[1], width) == (box >> BOX_BITS), 1.0)
            left[b, :, at] = owned
            left[b, :, low_at] = owned
            inside = places(BOX_DEV, width) == (box & (BOX_DEV - 1))
            for k in range(3):
                high, low = halves(picked[k][:, at] * weight)
                band = slice(k * BOX_DEV, (k + 1) * BOX_DEV)
                right[b, band, at] = marked(inside, high)
                right[b, band, low_at] = marked(inside, low)

    def chunks(i, _):
        own = [i * SIDE + b for b in range(SIDE)]
        spans = [windows(ends, j) for j in own]
        firsts = [window(own[b], b, spans[b][0], 0) for b in range(SIDE)]
        finals = []
        for b in range(SIDE):

            def more(w, picked, b=b):
                fresh = window(own[b], b, spans[b][0], w)
                return tuple(old + new for old, new in zip(picked, fresh))

            finals.append(lax.fori_loop(1, spans[b][1], more, firsts[b]))
        for b in range(SIDE):
            spread(own[b], b, finals[b])
        parts = [dot_last(right[b], left[b]) for b in range(SIDE)]
        total[...] += sum(parts[1:], parts[0])
        return 0

    lax.fori_loop(filled(ends), lines // group // SIDE, chunks, 0)
    for p in range(2):
        sums[:, p, :] = total[p * 128 : (p + 1) * 128, :].T
    out.wait()


def gather(ends, swept_from, cells, weights, boxes, devices):
    _, size_x, size_y, depth = swept_from[0].shape
    cube = (3, size_x * size_y, depth)
    vmem = pl.BlockSpec(memory_space=pltpu.VMEM)
    return pl.pallas_call(
        gather_kernel,
        in_specs=[pl.BlockSpec(memory_space=pltpu.SMEM)] + [vmem] * (len(swept_from) + 3),
        out_specs=[pl.BlockSpec(memory_space=pltpu.HBM), vmem],
        out_shape=[
            jax.ShapeDtypeStruct(cube, jnp.float32),
            jax.ShapeDtypeStruct((devices, 2, 128), jnp.float32),
        ],
        scratch_shapes=[
            pltpu.VMEM((3, size_x + 2, size_y, depth), jnp.float32),
            pltpu.VMEM(cube, jnp.float32),
            pltpu.VMEM((SIDE, 4 * WINDOW, STEP_ROWS), jnp.bfloat16),
            pltpu.VMEM((SIDE, devices, 2 * STEP_ROWS), jnp.bfloat16),
            pltpu.VMEM((SIDE, 4 * BOX_DEV, 2 * STEP_ROWS), jnp.bfloat16),
            pltpu.VMEM((4 * BOX_DEV, devices), jnp.float32),
            pltpu.SemaphoreType.DMA,
        ],
        compiler_params=pltpu.CompilerParams(vmem_limit_bytes=32 * MIB),
        name="gather_rows",
    )(ends, *swept_from, cells, weights, boxes)


def swapped(blocks):
    return lax.all_to_all(blocks, AXES, split_axis=0, concat_axis=0, tiled=True)


def body(
    sensitivity,
    node_weight,
    dest_device,
    dest_cell,
    box_owner,
    box_slot,
    stiffness,
    anchor,
    coupling,
):
    devices = lax.axis_size("gx") * lax.axis_size("gy")
    count = sensitivity.shape[1]
    size_x, size_y, size_z = stiffness.shape
    lane = lambda values: values.reshape(1, count)
    rows = pack(
        devices,
        sensitivity,
        lane(node_weight),
        lane(dest_device),
        lane(dest_cell),
        lane(box_owner),
        lane(box_slot),
    )
    rows = swapped(rows)
    planes = [rows[:, p].reshape(-1) for p in range(6)]
    keys = jnp.maximum(planes[3].astype(jnp.int32) - CELL_SHIFT, -1)
    ordered = lax.sort((keys, *planes[:3], *planes[4:]), num_keys=1, is_stable=False)
    cells, *values, weights, boxes = [part.reshape(-1, 128) for part in ordered]
    blocks = cells.reshape(-1, STEP_ROWS // 128, 128)
    ends = jnp.stack([blocks[:, 0, 0], blocks[:, -1, -1]])
    fixed, faces = scatter(ends, cells, values, stiffness, anchor, coupling)
    field = fixed[0]
    for turn in range(1, SWEEPS - 1):
        field, *faces = sweep(*fixed, field, *exchange(*faces))
    swept_from = (*fixed, field, *exchange(*faces))
    field, partial = gather(ends, swept_from, cells, weights, boxes, devices)
    field = field.reshape(3, size_x, size_y, size_z)
    summed = jnp.sum(swapped(partial), axis=0).reshape(4, BOX_DEV)
    return (field, summed[:3])


def solution(mesh):
    placed = (
        P(None, AXES),
        P(AXES),
        P(AXES, None),
        P(AXES),
        P(AXES, None),
        P(AXES),
        P("gx", "gy", None),
        P(None, "gx", "gy", None),
        P(None, "gx", "gy", None),
    )
    return jax.shard_map(
        body,
        mesh=mesh,
        in_specs=placed,
        out_specs=(P(None, "gx", "gy", None), P(None, AXES)),
        check_vma=False,
    )
```

```python
import jax
import jax.numpy as jnp
from jax import lax
from jax.experimental import pallas as pl
from jax.experimental.pallas import tpu as pltpu
from jax.sharding import PartitionSpec as P

BOX_DEV = 64
BOX_BITS = 6
SWEEPS = 4
AXES = ("gx", "gy")
STEP_ROWS = 512
RANK_ROWS = 256
WINDOW = 32
SIDE = 8
PARTS = 4
CELL_SHIFT = 257
KEY_BITS = 13
MIB = 1024 * 1024


def dot_last(left, right):
    return lax.dot_general(
        left, right, (((1,), (1,)), ((), ())), preferred_element_type=jnp.float32
    )


def halves(values):
    high = values.astype(jnp.bfloat16).astype(jnp.float32)
    return high, values - high


def places(height, width):
    return lax.broadcasted_iota(jnp.int32, (height, width), 0)


def marked(mask, row):
    return jnp.where(mask, row, 0.0).astype(jnp.bfloat16)


def pack_kernel(*refs):
    given, rows, kept = refs[:6], refs[6], refs[7:13]
    ranks, upper, left, right, total, arrivals = refs[13:]
    sens, weight, device, cell, owner, slot = kept
    devices, _, capacity = rows.shape
    half = capacity // 2
    part = upper.shape[0]
    step = STEP_ROWS
    steps = sens.shape[1] // step
    copies = [
        pltpu.make_async_copy(given[p], kept[p], arrivals.at[p]) for p in range(len(given))
    ]
    for copy in copies:
        copy.start()
    before = lax.broadcasted_iota(jnp.int32, (part, part), 0)
    after = lax.broadcasted_iota(jnp.int32, (part, part), 1)
    upper[...] = marked(before < after, 1.0)
    total[...] = jnp.zeros_like(total)
    for copy in copies:
        copy.wait()

    def rank(i, base):
        for b in range(4):
            at = pl.ds(pl.multiple_of((i * 4 + b) * part, part), part)
            here = places(devices, part) == device[:, at]
            ones = jnp.where(here, 1.0, 0.0)
            within = jnp.dot(
                ones.astype(jnp.bfloat16), upper[...], preferred_element_type=jnp.float32
            )
            ranks[:, at] = jnp.sum(
                jnp.where(here, within + base, 0.0), axis=0, keepdims=True
            ).astype(jnp.int32)
            base = base + jnp.sum(ones, axis=1, keepdims=True)
        return base

    lax.fori_loop(0, sens.shape[1] // part // 4, rank, jnp.zeros((devices, 1), jnp.float32))

    def chunk(i, _):
        for b in range(4):
            at = pl.ds(pl.multiple_of((i * 4 + b) * step, step), step)
            rank = ranks[:, at]
            lane = device[:, at] + jnp.where(rank >= half, devices, 0)
            ones = marked(places(2 * devices, step) == lane, 1.0)
            left[b, :, :step] = ones
            left[b, :, step:] = ones
            here = places(half, step) == (rank & (half - 1))
            own_cell = cell[:, at]
            pairs = [halves(sens[k : k + 1, at]) for k in range(3)]
            pairs.append(
                (
                    (((own_cell >> 9) + 1) << 9).astype(jnp.float32),
                    ((own_cell & 511) + (CELL_SHIFT - 512)).astype(jnp.float32),
                )
            )
            pairs.append(halves(weight[:, at]))
            pairs.append(
                ((owner[:, at] * BOX_DEV).astype(jnp.float32), slot[:, at].astype(jnp.float32))
            )
            for p, (high, low) in enumerate(pairs):
                band = slice(p * half, (p + 1) * half)
                right[b, band, :step] = marked(here, high)
                right[b, band, step:] = marked(here, low)
        total[...] += sum(dot_last(right[b], left[b]) for b in range(4))
        return 0

    lax.fori_loop(0, steps // 4, chunk, 0)
    for p in range(6):
        band = total[p * half : (p + 1) * half, :]
        rows[:, p, :] = jnp.concatenate([band[:, :devices].T, band[:, devices:].T], axis=1)
    for p in range(6, 8):
        rows[:, p, :] = jnp.zeros((devices, capacity), jnp.float32)


def pack(devices, *given):
    count = given[0].shape[1]
    capacity = 2 * count // devices
    return pl.pallas_call(
        pack_kernel,
        in_specs=[pl.BlockSpec(memory_space=pltpu.HBM)] * len(given),
        out_shape=jax.ShapeDtypeStruct((devices, 8, capacity), jnp.float32),
        scratch_shapes=[pltpu.VMEM(part.shape, part.dtype) for part in given]
        + [
            pltpu.VMEM((1, count), jnp.int32),
            pltpu.VMEM((RANK_ROWS, RANK_ROWS), jnp.bfloat16),
            pltpu.VMEM((4, 2 * devices, 2 * STEP_ROWS), jnp.bfloat16),
            pltpu.VMEM((4, 3 * capacity, 2 * STEP_ROWS), jnp.bfloat16),
            pltpu.VMEM((3 * capacity, 2 * devices), jnp.float32),
            pltpu.SemaphoreType.DMA((len(given),)),
        ],
        compiler_params=pltpu.CompilerParams(vmem_limit_bytes=58 * MIB),
        name="pack_rows",
    )(*given)


def windows(ends, i):
    first = jnp.maximum(ends[0, i] >> 8, 0)
    start = first & ~7
    return start, (jnp.maximum((ends[1, i] >> 8) + WINDOW - start, 0)) // WINDOW


def filled(ends):
    groups = ends.shape[1] // SIDE

    def count(g, empty):
        return empty + jnp.where(ends[1, g * SIDE + SIDE - 1] < 0, 1, 0)

    return lax.fori_loop(0, groups, count, 0)


def scatter_kernel(*refs):
    ends, cells, one, two, three, stiff_at, anchor_at, coupling_at = refs[:8]
    load, scaled, inverse, stiff, head_x, tail_x, head_y, tail_y = refs[8:16]
    anchor, coupling, left, right, arrivals = refs[16:]
    copies = [
        pltpu.make_async_copy(source, target, arrivals.at[p])
        for p, (source, target) in enumerate(
            ((stiff_at, stiff), (anchor_at, anchor), (coupling_at, coupling))
        )
    ]
    for copy in copies:
        copy.start()
    height, depth = load.shape[1:]
    lines, width = cells.shape
    part = depth // PARTS
    group = STEP_ROWS // width
    step = STEP_ROWS
    load[...] = jnp.zeros_like(load)

    def fill(i, b):
        for q in range(group):
            row = pl.ds(i * group + q, 1)
            there = places(part, width) == ((cells[row, :] >> KEY_BITS) & (part - 1))
            for k, sens in enumerate((one, two, three)):
                high, low = halves(sens[row, :])
                band = slice(k * part, (k + 1) * part)
                right[b, band, q * width : (q + 1) * width] = marked(there, high)
                right[b, band, step + q * width : step + (q + 1) * width] = marked(there, low)

    def window(i, b, start, w):
        least = start + w * WINDOW
        base = pl.multiple_of(jnp.minimum(least, height - WINDOW), 8)
        for q in range(group):
            cell = cells[pl.ds(i * group + q, 1), :] >> KEY_BITS
            place = window_place(cell, least, base, PARTS)
            hot = marked(places(PARTS * WINDOW, width) == place, 1.0)
            left[b, :, q * width : (q + 1) * width] = hot
            left[b, :, step + q * width : step + (q + 1) * width] = hot
        sums = dot_last(left[b], right[b])

        def add():
            for k in range(3):
                for side in range(PARTS // 2):
                    at = (k, pl.ds(base, WINDOW), slice(side * 2 * part, (side + 1) * 2 * part))
                    load[at] += jnp.concatenate(
                        [
                            sums[p * WINDOW : (p + 1) * WINDOW, k * part : (k + 1) * part]
                            for p in (2 * side, 2 * side + 1)
                        ],
                        axis=1,
                    )

        return add

    def chunks(i, _):
        own = [i * SIDE + b for b in range(SIDE)]
        spans = [windows(ends, j) for j in own]
        for b in range(SIDE):
            fill(own[b], b)
        adds = [window(own[b], b, spans[b][0], 0) for b in range(SIDE)]
        for add in adds:
            add()
        for b in range(SIDE):

            def more(w, _, b=b):
                window(own[b], b, spans[b][0], w)()
                return 0

            lax.fori_loop(1, spans[b][1], more, 0)
        return 0

    lax.fori_loop(filled(ends), lines // group // SIDE, chunks, 0)
    for copy in copies:
        copy.wait()
    size_x, size_y = head_y.shape[1], head_x.shape[1]
    for x in range(size_x):
        at = slice(x * size_y, (x + 1) * size_y)
        weight = stiff[at]
        for k in range(3):
            own = 1.0 / (6.0 * weight + anchor[k, at] + coupling[4 * k, at])
            inverse[k, at] = own
            for place, j in enumerate(others(k)):
                scaled[2 * k + place, at] = coupling[3 * j + k, at] * own
            fresh = load[k, at] * own
            load[k, at] = fresh
            moved = weight * fresh
            if x == 0:
                head_x[k] = moved
            if x == size_x - 1:
                tail_x[k] = moved
            head_y[k, x : x + 1] = moved[:1]
            tail_y[k, x : x + 1] = moved[size_y - 1 :]


def window_place(cell, least, base, parts):
    line = cell >> 8
    place = ((cell & 255) * parts >> 8) * WINDOW + line - base
    inside = (line >= least) & (line < base + WINDOW)
    return jnp.where(inside, place, -1)


def scatter(ends, cells, values, stiff, anchor, coupling):
    size_x, size_y, depth = stiff.shape
    height = size_x * size_y
    vmem = pl.BlockSpec(memory_space=pltpu.VMEM)
    shapes = [(3, height, depth), (6, height, depth), (3, height, depth), (height, depth)]
    shapes += [(3, size_y, depth)] * 2 + [(3, size_x, depth)] * 2
    outs = pl.pallas_call(
        scatter_kernel,
        in_specs=[pl.BlockSpec(memory_space=pltpu.SMEM)]
        + [vmem] * 4
        + [pl.BlockSpec(memory_space=pltpu.HBM)] * 3,
        out_specs=[vmem] * 8,
        out_shape=[jax.ShapeDtypeStruct(shape, jnp.float32) for shape in shapes],
        scratch_shapes=[
            pltpu.VMEM((3, height, depth), jnp.float32),
            pltpu.VMEM((9, height, depth), jnp.float32),
            pltpu.VMEM((SIDE, PARTS * WINDOW, 2 * STEP_ROWS), jnp.bfloat16),
            pltpu.VMEM((SIDE, 3 * depth // PARTS, 2 * STEP_ROWS), jnp.bfloat16),
            pltpu.SemaphoreType.DMA((3,)),
        ],
        compiler_params=pltpu.CompilerParams(vmem_limit_bytes=41 * MIB),
        name="scatter_rows",
    )(
        ends,
        cells,
        *values,
        *(part.reshape(*part.shape[:-3], height, depth) for part in (stiff, anchor, coupling)),
    )
    cells_of = [part.reshape(*part.shape[:-2], size_x, size_y, depth) for part in outs[:4]]
    return cells_of, outs[4:]


def swept(first, scaled, inverse, stiff, field, halo, padded, store):
    _, size_x, size_y, size_z = field.shape
    south, north, west, east = halo
    padded[:, 0] = west[...]
    padded[:, size_x + 1] = east[...]
    for x in range(size_x):
        for k in range(3):
            padded[k, x + 1] = stiff[x] * field[k, x]
    row = lax.broadcasted_iota(jnp.int32, (size_y, size_z), 0)
    column = lax.broadcasted_iota(jnp.int32, (size_y, size_z), 1)
    for x in range(size_x):
        own = [field[k, x] for k in range(3)]
        for k in range(3):
            middle = padded[k, x + 1]
            total = padded[k, x] + padded[k, x + 2]
            total = total + jnp.where(row == 0, south[k, x : x + 1], pltpu.roll(middle, 1, 0))
            total = total + jnp.where(
                row == size_y - 1, north[k, x : x + 1], pltpu.roll(middle, size_y - 1, 0)
            )
            total = total + jnp.where(column == 0, 0.0, pltpu.roll(middle, 1, 1))
            total = total + jnp.where(
                column == size_z - 1, 0.0, pltpu.roll(middle, size_z - 1, 1)
            )
            fresh = first[k, x] + total * inverse[k, x]
            for place, j in enumerate(others(k)):
                fresh = fresh - scaled[2 * k + place, x] * own[j]
            store(k, x, fresh)


def others(k):
    return [j for j in range(3) if j != k]


def sweep_kernel(first, scaled, inverse, stiff, field, south, north, west, east, *outs):
    result, head_x, tail_x, head_y, tail_y, padded = outs
    size_x, size_y = field.shape[1:3]

    def store(k, x, fresh):
        result[k, x] = fresh
        moved = stiff[x] * fresh
        if x == 0:
            head_x[k] = moved
        if x == size_x - 1:
            tail_x[k] = moved
        head_y[k, x : x + 1] = moved[:1]
        tail_y[k, x : x + 1] = moved[size_y - 1 :]

    swept(first, scaled, inverse, stiff, field, (south, north, west, east), padded, store)


def sweep(*given):
    _, size_x, size_y, size_z = given[0].shape
    shapes = [given[0].shape] + [(3, size_y, size_z)] * 2 + [(3, size_x, size_z)] * 2
    return pl.pallas_call(
        sweep_kernel,
        out_shape=[jax.ShapeDtypeStruct(shape, jnp.float32) for shape in shapes],
        scratch_shapes=[pltpu.VMEM((3, size_x + 2, size_y, size_z), jnp.float32)],
        compiler_params=pltpu.CompilerParams(vmem_limit_bytes=8 * MIB),
        name="sweep_cells",
    )(*given)


def exchange(head_x, tail_x, head_y, tail_y):
    def shifted(face, axis, up):
        pairs = [(i, i + 1) if up else (i + 1, i) for i in range(lax.axis_size(axis) - 1)]
        return lax.ppermute(face, axis, pairs)

    south = shifted(tail_y, "gy", True)
    north = shifted(head_y, "gy", False)
    west = shifted(tail_x, "gx", True)
    east = shifted(head_x, "gx", False)
    return south, north, west, east


def gather_kernel(*refs):
    ends, first, scaled, inverse, stiff, before, south, north, west, east = refs[:10]
    cells, weights, final, sums, padded, field, hot, left, right, total, sent = refs[10:]
    size_y = before.shape[2]

    def store(k, x, fresh):
        field[k, x * size_y : (x + 1) * size_y] = fresh

    swept(first, scaled, inverse, stiff, before, (south, north, west, east), padded, store)
    out = pltpu.make_async_copy(field, final, sent)
    out.start()
    height, depth = field.shape[1:]
    lines, width = cells.shape
    half = depth // 2
    group = STEP_ROWS // width
    step = STEP_ROWS
    total[...] = jnp.zeros_like(total)
    right[...] = jnp.zeros_like(right)

    def rows(i):
        return [pl.ds(i * group + q, 1) for q in range(group)]

    def window(i, b, start, w):
        least = start + w * WINDOW
        base = pl.multiple_of(jnp.minimum(least, height - WINDOW), 8)
        own = [cells[row, :] >> KEY_BITS for row in rows(i)]
        for q in range(group):
            ones = marked(places(2 * WINDOW, width) == window_place(own[q], least, base, 2), 1.0)
            hot[b, : 2 * WINDOW, q * width : (q + 1) * width] = ones
            hot[b, 2 * WINDOW :, q * width : (q + 1) * width] = ones
        there = [places(half, width) == (cell & (half - 1)) for cell in own]
        picked = []
        block = jnp.concatenate(
            [
                jnp.concatenate(
                    [field[k, pl.ds(base, WINDOW), side * half : (side + 1) * half] for k in range(3)],
                    axis=1,
                )
                for side in range(2)
            ],
            axis=0,
        )
        both = jnp.concatenate(halves(block), axis=0).T.astype(jnp.bfloat16)
        parts = jnp.dot(both, hot[b], preferred_element_type=jnp.float32)
        for k in range(3):
            part = parts[k * half : (k + 1) * half]
            picked.append(
                jnp.concatenate(
                    [
                        jnp.sum(
                            jnp.where(there[q], part[:, q * width : (q + 1) * width], 0.0),
                            axis=0,
                            keepdims=True,
                        )
                        for q in range(group)
                    ],
                    axis=1,
                )
            )
        return tuple(picked)

    def spread(i, b, picked):
        for q, row in enumerate(rows(i)):
            at = slice(q * width, (q + 1) * width)
            low_at = slice(step + q * width, step + (q + 1) * width)
            weight = weights[row, :]
            box = cells[row, :] & (2**KEY_BITS - 1)
            owned = marked(places(left.shape[1], width) == (box >> BOX_BITS), 1.0)
            left[b, :, at] = owned
            left[b, :, low_at] = owned
            inside = places(BOX_DEV, width) == (box & (BOX_DEV - 1))
            for k in range(3):
                high, low = halves(picked[k][:, at] * weight)
                band = slice(k * BOX_DEV, (k + 1) * BOX_DEV)
                right[b, band, at] = marked(inside, high)
                right[b, band, low_at] = marked(inside, low)

    def chunks(i, _):
        own = [i * SIDE + b for b in range(SIDE)]
        spans = [windows(ends, j) for j in own]
        firsts = [window(own[b], b, spans[b][0], 0) for b in range(SIDE)]
        finals = []
        for b in range(SIDE):

            def more(w, picked, b=b):
                fresh = window(own[b], b, spans[b][0], w)
                return tuple(old + new for old, new in zip(picked, fresh))

            finals.append(lax.fori_loop(1, spans[b][1], more, firsts[b]))
        for b in range(SIDE):
            spread(own[b], b, finals[b])
        parts = [dot_last(right[b], left[b]) for b in range(SIDE)]
        total[...] += sum(parts[1:], parts[0])
        return 0

    lax.fori_loop(filled(ends), lines // group // SIDE, chunks, 0)
    for p in range(2):
        sums[:, p, :] = total[p * 128 : (p + 1) * 128, :].T
    out.wait()


def gather(ends, swept_from, cells, weights, devices):
    _, size_x, size_y, depth = swept_from[0].shape
    cube = (3, size_x * size_y, depth)
    vmem = pl.BlockSpec(memory_space=pltpu.VMEM)
    return pl.pallas_call(
        gather_kernel,
        in_specs=[pl.BlockSpec(memory_space=pltpu.SMEM)] + [vmem] * (len(swept_from) + 2),
        out_specs=[pl.BlockSpec(memory_space=pltpu.HBM), vmem],
        out_shape=[
            jax.ShapeDtypeStruct(cube, jnp.float32),
            jax.ShapeDtypeStruct((devices, 2, 128), jnp.float32),
        ],
        scratch_shapes=[
            pltpu.VMEM((3, size_x + 2, size_y, depth), jnp.float32),
            pltpu.VMEM(cube, jnp.float32),
            pltpu.VMEM((SIDE, 4 * WINDOW, STEP_ROWS), jnp.bfloat16),
            pltpu.VMEM((SIDE, devices, 2 * STEP_ROWS), jnp.bfloat16),
            pltpu.VMEM((SIDE, 4 * BOX_DEV, 2 * STEP_ROWS), jnp.bfloat16),
            pltpu.VMEM((4 * BOX_DEV, devices), jnp.float32),
            pltpu.SemaphoreType.DMA,
        ],
        compiler_params=pltpu.CompilerParams(vmem_limit_bytes=32 * MIB),
        name="gather_rows",
    )(ends, *swept_from, cells, weights)


def swapped(blocks):
    return lax.all_to_all(blocks, AXES, split_axis=0, concat_axis=0, tiled=True)


def body(
    sensitivity,
    node_weight,
    dest_device,
    dest_cell,
    box_owner,
    box_slot,
    stiffness,
    anchor,
    coupling,
):
    devices = lax.axis_size("gx") * lax.axis_size("gy")
    count = sensitivity.shape[1]
    size_x, size_y, size_z = stiffness.shape
    lane = lambda values: values.reshape(1, count)
    rows = pack(
        devices,
        sensitivity,
        lane(node_weight),
        lane(dest_device),
        lane(dest_cell),
        lane(box_owner),
        lane(box_slot),
    )
    rows = swapped(rows)
    planes = [rows[:, p].reshape(-1) for p in range(6)]
    found = (planes[3].astype(jnp.int32) - CELL_SHIFT) << KEY_BITS
    keys = jnp.maximum(found + planes[5].astype(jnp.int32), -1)
    ordered = lax.sort((keys, *planes[:3], planes[4]), num_keys=1, is_stable=False)
    cells, *values, weights = [part.reshape(-1, 128) for part in ordered]
    blocks = cells.reshape(-1, STEP_ROWS // 128, 128)
    ends = jnp.stack([blocks[:, 0, 0], blocks[:, -1, -1]]) >> KEY_BITS
    fixed, faces = scatter(ends, cells, values, stiffness, anchor, coupling)
    field = fixed[0]
    for turn in range(1, SWEEPS - 1):
        field, *faces = sweep(*fixed, field, *exchange(*faces))
    swept_from = (*fixed, field, *exchange(*faces))
    field, partial = gather(ends, swept_from, cells, weights, devices)
    field = field.reshape(3, size_x, size_y, size_z)
    summed = jnp.sum(swapped(partial), axis=0).reshape(4, BOX_DEV)
    return (field, summed[:3])


def solution(mesh):
    placed = (
        P(None, AXES),
        P(AXES),
        P(AXES, None),
        P(AXES),
        P(AXES, None),
        P(AXES),
        P("gx", "gy", None),
        P(None, "gx", "gy", None),
        P(None, "gx", "gy", None),
    )
    return jax.shard_map(
        body,
        mesh=mesh,
        in_specs=placed,
        out_specs=(P(None, "gx", "gy", None), P(None, AXES)),
        check_vma=False,
    )
```

```python
import jax
import jax.numpy as jnp
from jax import lax
from jax.experimental import pallas as pl
from jax.experimental.pallas import tpu as pltpu
from jax.sharding import PartitionSpec as P

BOX_DEV = 64
BOX_BITS = 6
SWEEPS = 4
AXES = ("gx", "gy")
STEP_ROWS = 512
RANK_ROWS = 256
WINDOW = 32
SIDE = 8
PARTS = 4
CELL_SHIFT = 257
KEY_BITS = 13
MIB = 1024 * 1024


def dot_last(left, right):
    return lax.dot_general(
        left, right, (((1,), (1,)), ((), ())), preferred_element_type=jnp.float32
    )


def halves(values):
    high = values.astype(jnp.bfloat16).astype(jnp.float32)
    return high, values - high


def places(height, width):
    return lax.broadcasted_iota(jnp.int32, (height, width), 0)


def marked(mask, row):
    return jnp.where(mask, row, 0.0).astype(jnp.bfloat16)


def pack_kernel(*refs):
    given, rows, kept = refs[:6], refs[6], refs[7:13]
    ranks, upper, left, right, total, arrivals = refs[13:]
    sens, weight, device, cell, owner, slot = kept
    devices, _, capacity = rows.shape
    half = capacity // 2
    part = upper.shape[0]
    step = STEP_ROWS
    steps = sens.shape[1] // step
    copies = [
        pltpu.make_async_copy(given[p], kept[p], arrivals.at[p]) for p in range(len(given))
    ]
    for copy in copies:
        copy.start()
    before = lax.broadcasted_iota(jnp.int32, (part, part), 0)
    after = lax.broadcasted_iota(jnp.int32, (part, part), 1)
    upper[...] = marked(before < after, 1.0)
    total[...] = jnp.zeros_like(total)
    for copy in copies:
        copy.wait()

    def rank(i, base):
        for b in range(4):
            at = pl.ds(pl.multiple_of((i * 4 + b) * part, part), part)
            here = places(devices, part) == device[:, at]
            ones = jnp.where(here, 1.0, 0.0)
            within = jnp.dot(
                ones.astype(jnp.bfloat16), upper[...], preferred_element_type=jnp.float32
            )
            ranks[:, at] = jnp.sum(
                jnp.where(here, within + base, 0.0), axis=0, keepdims=True
            ).astype(jnp.int32)
            base = base + jnp.sum(ones, axis=1, keepdims=True)
        return base

    lax.fori_loop(0, sens.shape[1] // part // 4, rank, jnp.zeros((devices, 1), jnp.float32))

    def chunk(i, _):
        for b in range(4):
            at = pl.ds(pl.multiple_of((i * 4 + b) * step, step), step)
            rank = ranks[:, at]
            lane = device[:, at] + jnp.where(rank >= half, devices, 0)
            ones = marked(places(2 * devices, step) == lane, 1.0)
            left[b, :, :step] = ones
            left[b, :, step:] = ones
            here = places(half, step) == (rank & (half - 1))
            own_cell = cell[:, at]
            pairs = [halves(sens[k : k + 1, at]) for k in range(3)]
            pairs.append(
                (
                    (((own_cell >> 9) + 1) << 9).astype(jnp.float32),
                    ((own_cell & 511) + (CELL_SHIFT - 512)).astype(jnp.float32),
                )
            )
            pairs.append(halves(weight[:, at]))
            pairs.append(
                ((owner[:, at] * BOX_DEV).astype(jnp.float32), slot[:, at].astype(jnp.float32))
            )
            for p, (high, low) in enumerate(pairs):
                band = slice(p * half, (p + 1) * half)
                right[b, band, :step] = marked(here, high)
                right[b, band, step:] = marked(here, low)
        total[...] += sum(dot_last(right[b], left[b]) for b in range(4))
        return 0

    lax.fori_loop(0, steps // 4, chunk, 0)
    for p in range(6):
        band = total[p * half : (p + 1) * half, :]
        rows[:, p, :] = jnp.concatenate([band[:, :devices].T, band[:, devices:].T], axis=1)
    for p in range(6, 8):
        rows[:, p, :] = jnp.zeros((devices, capacity), jnp.float32)


def pack(devices, *given):
    count = given[0].shape[1]
    capacity = 2 * count // devices
    return pl.pallas_call(
        pack_kernel,
        in_specs=[pl.BlockSpec(memory_space=pltpu.HBM)] * len(given),
        out_shape=jax.ShapeDtypeStruct((devices, 8, capacity), jnp.float32),
        scratch_shapes=[pltpu.VMEM(part.shape, part.dtype) for part in given]
        + [
            pltpu.VMEM((1, count), jnp.int32),
            pltpu.VMEM((RANK_ROWS, RANK_ROWS), jnp.bfloat16),
            pltpu.VMEM((4, 2 * devices, 2 * STEP_ROWS), jnp.bfloat16),
            pltpu.VMEM((4, 3 * capacity, 2 * STEP_ROWS), jnp.bfloat16),
            pltpu.VMEM((3 * capacity, 2 * devices), jnp.float32),
            pltpu.SemaphoreType.DMA((len(given),)),
        ],
        compiler_params=pltpu.CompilerParams(vmem_limit_bytes=58 * MIB),
        name="pack_rows",
    )(*given)


def windows(ends, i):
    first = jnp.maximum(ends[0, i] >> 8, 0)
    start = first & ~7
    return start, (jnp.maximum((ends[1, i] >> 8) + WINDOW - start, 0)) // WINDOW


def filled(ends):
    groups = ends.shape[1] // SIDE

    def count(g, empty):
        return empty + jnp.where(ends[1, g * SIDE + SIDE - 1] < 0, 1, 0)

    return lax.fori_loop(0, groups, count, 0)


def scatter_kernel(*refs):
    ends, cells, one, two, three, stiff_at, anchor_at, coupling_at = refs[:8]
    load, scaled, inverse, stiff, head_x, tail_x, head_y, tail_y = refs[8:16]
    anchor, coupling, left, right, arrivals = refs[16:]
    copies = [
        pltpu.make_async_copy(source, target, arrivals.at[p])
        for p, (source, target) in enumerate(
            ((stiff_at, stiff), (anchor_at, anchor), (coupling_at, coupling))
        )
    ]
    for copy in copies:
        copy.start()
    height, depth = load.shape[1:]
    lines, width = cells.shape
    part = depth // PARTS
    group = STEP_ROWS // width
    step = STEP_ROWS
    load[...] = jnp.zeros_like(load)

    def fill(i, b):
        for q in range(group):
            row = pl.ds(i * group + q, 1)
            there = places(part, width) == ((cells[row, :] >> KEY_BITS) & (part - 1))
            for k, sens in enumerate((one, two, three)):
                high, low = halves(sens[row, :])
                band = slice(k * part, (k + 1) * part)
                right[b, band, q * width : (q + 1) * width] = marked(there, high)
                right[b, band, step + q * width : step + (q + 1) * width] = marked(there, low)

    def window(i, b, start, w):
        least = start + w * WINDOW
        base = pl.multiple_of(jnp.minimum(least, height - WINDOW), 8)
        for q in range(group):
            cell = cells[pl.ds(i * group + q, 1), :] >> KEY_BITS
            place = window_place(cell, least, base, PARTS)
            hot = marked(places(PARTS * WINDOW, width) == place, 1.0)
            left[b, :, q * width : (q + 1) * width] = hot
            left[b, :, step + q * width : step + (q + 1) * width] = hot
        sums = dot_last(left[b], right[b])

        def add():
            for k in range(3):
                for side in range(PARTS // 2):
                    at = (k, pl.ds(base, WINDOW), slice(side * 2 * part, (side + 1) * 2 * part))
                    load[at] += jnp.concatenate(
                        [
                            sums[p * WINDOW : (p + 1) * WINDOW, k * part : (k + 1) * part]
                            for p in (2 * side, 2 * side + 1)
                        ],
                        axis=1,
                    )

        return add

    def chunks(i, _):
        own = [i * SIDE + b for b in range(SIDE)]
        spans = [windows(ends, j) for j in own]
        for b in range(SIDE):
            fill(own[b], b)
        adds = [window(own[b], b, spans[b][0], 0) for b in range(SIDE)]
        for add in adds:
            add()
        for b in range(SIDE):

            def more(w, _, b=b):
                window(own[b], b, spans[b][0], w)()
                return 0

            lax.fori_loop(1, spans[b][1], more, 0)
        return 0

    lax.fori_loop(filled(ends), lines // group // SIDE, chunks, 0)
    for copy in copies:
        copy.wait()
    size_x, size_y = head_y.shape[1], head_x.shape[1]
    for x in range(size_x):
        at = slice(x * size_y, (x + 1) * size_y)
        weight = stiff[at]
        for k in range(3):
            own = 1.0 / (6.0 * weight + anchor[k, at] + coupling[4 * k, at])
            inverse[k, at] = own
            for place, j in enumerate(others(k)):
                scaled[2 * k + place, at] = coupling[3 * j + k, at] * own
            fresh = load[k, at] * own
            load[k, at] = fresh
            moved = weight * fresh
            if x == 0:
                head_x[k] = moved
            if x == size_x - 1:
                tail_x[k] = moved
            head_y[k, x : x + 1] = moved[:1]
            tail_y[k, x : x + 1] = moved[size_y - 1 :]


def window_place(cell, least, base, parts):
    line = cell >> 8
    place = ((cell & 255) * parts >> 8) * WINDOW + line - base
    inside = (line >= least) & (line < base + WINDOW)
    return jnp.where(inside, place, -1)


def scatter(ends, cells, values, stiff, anchor, coupling):
    size_x, size_y, depth = stiff.shape
    height = size_x * size_y
    vmem = pl.BlockSpec(memory_space=pltpu.VMEM)
    shapes = [(3, height, depth), (6, height, depth), (3, height, depth), (height, depth)]
    shapes += [(3, size_y, depth)] * 2 + [(3, size_x, depth)] * 2
    outs = pl.pallas_call(
        scatter_kernel,
        in_specs=[pl.BlockSpec(memory_space=pltpu.SMEM)]
        + [vmem] * 4
        + [pl.BlockSpec(memory_space=pltpu.HBM)] * 3,
        out_specs=[vmem] * 8,
        out_shape=[jax.ShapeDtypeStruct(shape, jnp.float32) for shape in shapes],
        scratch_shapes=[
            pltpu.VMEM((3, height, depth), jnp.float32),
            pltpu.VMEM((9, height, depth), jnp.float32),
            pltpu.VMEM((SIDE, PARTS * WINDOW, 2 * STEP_ROWS), jnp.bfloat16),
            pltpu.VMEM((SIDE, 3 * depth // PARTS, 2 * STEP_ROWS), jnp.bfloat16),
            pltpu.SemaphoreType.DMA((3,)),
        ],
        compiler_params=pltpu.CompilerParams(vmem_limit_bytes=41 * MIB),
        name="scatter_rows",
    )(
        ends,
        cells,
        *values,
        *(part.reshape(*part.shape[:-3], height, depth) for part in (stiff, anchor, coupling)),
    )
    cells_of = [part.reshape(*part.shape[:-2], size_x, size_y, depth) for part in outs[:4]]
    return cells_of, outs[4:]


def swept(first, scaled, inverse, stiff, field, halo, padded, store):
    _, size_x, size_y, size_z = field.shape
    south, north, west, east = halo
    padded[:, 0] = west[...]
    padded[:, size_x + 1] = east[...]
    for x in range(size_x):
        for k in range(3):
            padded[k, x + 1] = stiff[x] * field[k, x]
    row = lax.broadcasted_iota(jnp.int32, (size_y, size_z), 0)
    column = lax.broadcasted_iota(jnp.int32, (size_y, size_z), 1)
    for x in range(size_x):
        own = [field[k, x] for k in range(3)]
        for k in range(3):
            middle = padded[k, x + 1]
            total = padded[k, x] + padded[k, x + 2]
            total = total + jnp.where(row == 0, south[k, x : x + 1], pltpu.roll(middle, 1, 0))
            total = total + jnp.where(
                row == size_y - 1, north[k, x : x + 1], pltpu.roll(middle, size_y - 1, 0)
            )
            total = total + jnp.where(column == 0, 0.0, pltpu.roll(middle, 1, 1))
            total = total + jnp.where(
                column == size_z - 1, 0.0, pltpu.roll(middle, size_z - 1, 1)
            )
            fresh = first[k, x] + total * inverse[k, x]
            for place, j in enumerate(others(k)):
                fresh = fresh - scaled[2 * k + place, x] * own[j]
            store(k, x, fresh)


def others(k):
    return [j for j in range(3) if j != k]


def sweep_kernel(first, scaled, inverse, stiff, field, south, north, west, east, *outs):
    result, head_x, tail_x, head_y, tail_y, padded = outs
    size_x, size_y = field.shape[1:3]

    def store(k, x, fresh):
        result[k, x] = fresh
        moved = stiff[x] * fresh
        if x == 0:
            head_x[k] = moved
        if x == size_x - 1:
            tail_x[k] = moved
        head_y[k, x : x + 1] = moved[:1]
        tail_y[k, x : x + 1] = moved[size_y - 1 :]

    swept(first, scaled, inverse, stiff, field, (south, north, west, east), padded, store)


def sweep(*given):
    _, size_x, size_y, size_z = given[0].shape
    shapes = [given[0].shape] + [(3, size_y, size_z)] * 2 + [(3, size_x, size_z)] * 2
    return pl.pallas_call(
        sweep_kernel,
        out_shape=[jax.ShapeDtypeStruct(shape, jnp.float32) for shape in shapes],
        scratch_shapes=[pltpu.VMEM((3, size_x + 2, size_y, size_z), jnp.float32)],
        compiler_params=pltpu.CompilerParams(vmem_limit_bytes=8 * MIB),
        name="sweep_cells",
    )(*given)


def exchange(head_x, tail_x, head_y, tail_y):
    def shifted(face, axis, up):
        pairs = [(i, i + 1) if up else (i + 1, i) for i in range(lax.axis_size(axis) - 1)]
        return lax.ppermute(face, axis, pairs)

    south = shifted(tail_y, "gy", True)
    north = shifted(head_y, "gy", False)
    west = shifted(tail_x, "gx", True)
    east = shifted(head_x, "gx", False)
    return south, north, west, east


def gather_kernel(*refs):
    ends, first, scaled, inverse, stiff, before, south, north, west, east = refs[:10]
    cells, weights, final, sums, padded, field, hot, left, right, total, sent = refs[10:]
    size_y = before.shape[2]

    def store(k, x, fresh):
        field[k, x * size_y : (x + 1) * size_y] = fresh

    swept(first, scaled, inverse, stiff, before, (south, north, west, east), padded, store)
    out = pltpu.make_async_copy(field, final, sent)
    out.start()
    height, depth = field.shape[1:]
    lines, width = cells.shape
    half = depth // 2
    group = STEP_ROWS // width
    step = STEP_ROWS
    total[...] = jnp.zeros_like(total)
    right[...] = jnp.zeros_like(right)

    def rows(i):
        return [pl.ds(i * group + q, 1) for q in range(group)]

    def fill(i, b):
        for q, row in enumerate(rows(i)):
            place = (cells[row, :] >> KEY_BITS) & (half - 1)
            ones = marked(places(half, width) == place, 1.0)
            hot[b, :half, q * width : (q + 1) * width] = ones
            hot[b, half:, q * width : (q + 1) * width] = ones

    def window(i, b, start, w):
        least = start + w * WINDOW
        base = pl.multiple_of(jnp.minimum(least, height - WINDOW), 8)
        there = [
            places(2 * WINDOW, width)
            == window_place(cells[row, :] >> KEY_BITS, least, base, 2)
            for row in rows(i)
        ]
        block = jnp.concatenate(
            [
                field[k, pl.ds(base, WINDOW), side * half : (side + 1) * half]
                for k in range(3)
                for side in range(2)
            ],
            axis=0,
        )
        both = jnp.concatenate(halves(block), axis=1).astype(jnp.bfloat16)
        parts = jnp.dot(both, hot[b], preferred_element_type=jnp.float32)
        picked = []
        for k in range(3):
            part = parts[k * 2 * WINDOW : (k + 1) * 2 * WINDOW]
            picked.append(
                jnp.concatenate(
                    [
                        jnp.sum(
                            jnp.where(there[q], part[:, q * width : (q + 1) * width], 0.0),
                            axis=0,
                            keepdims=True,
                        )
                        for q in range(group)
                    ],
                    axis=1,
                )
            )
        return tuple(picked)

    def spread(i, b, picked):
        for q, row in enumerate(rows(i)):
            at = slice(q * width, (q + 1) * width)
            low_at = slice(step + q * width, step + (q + 1) * width)
            weight = weights[row, :]
            box = cells[row, :] & (2**KEY_BITS - 1)
            owned = marked(places(left.shape[1], width) == (box >> BOX_BITS), 1.0)
            left[b, :, at] = owned
            left[b, :, low_at] = owned
            inside = places(BOX_DEV, width) == (box & (BOX_DEV - 1))
            for k in range(3):
                high, low = halves(picked[k][:, at] * weight)
                band = slice(k * BOX_DEV, (k + 1) * BOX_DEV)
                right[b, band, at] = marked(inside, high)
                right[b, band, low_at] = marked(inside, low)

    def chunks(i, _):
        own = [i * SIDE + b for b in range(SIDE)]
        spans = [windows(ends, j) for j in own]
        for b in range(SIDE):
            fill(own[b], b)
        firsts = [window(own[b], b, spans[b][0], 0) for b in range(SIDE)]
        finals = []
        for b in range(SIDE):

            def more(w, picked, b=b):
                fresh = window(own[b], b, spans[b][0], w)
                return tuple(old + new for old, new in zip(picked, fresh))

            finals.append(lax.fori_loop(1, spans[b][1], more, firsts[b]))
        for b in range(SIDE):
            spread(own[b], b, finals[b])
        parts = [dot_last(right[b], left[b]) for b in range(SIDE)]
        total[...] += sum(parts[1:], parts[0])
        return 0

    lax.fori_loop(filled(ends), lines // group // SIDE, chunks, 0)
    for p in range(2):
        sums[:, p, :] = total[p * 128 : (p + 1) * 128, :].T
    out.wait()


def gather(ends, swept_from, cells, weights, devices):
    _, size_x, size_y, depth = swept_from[0].shape
    cube = (3, size_x * size_y, depth)
    vmem = pl.BlockSpec(memory_space=pltpu.VMEM)
    return pl.pallas_call(
        gather_kernel,
        in_specs=[pl.BlockSpec(memory_space=pltpu.SMEM)] + [vmem] * (len(swept_from) + 2),
        out_specs=[pl.BlockSpec(memory_space=pltpu.HBM), vmem],
        out_shape=[
            jax.ShapeDtypeStruct(cube, jnp.float32),
            jax.ShapeDtypeStruct((devices, 2, 128), jnp.float32),
        ],
        scratch_shapes=[
            pltpu.VMEM((3, size_x + 2, size_y, depth), jnp.float32),
            pltpu.VMEM(cube, jnp.float32),
            pltpu.VMEM((SIDE, depth, STEP_ROWS), jnp.bfloat16),
            pltpu.VMEM((SIDE, devices, 2 * STEP_ROWS), jnp.bfloat16),
            pltpu.VMEM((SIDE, 4 * BOX_DEV, 2 * STEP_ROWS), jnp.bfloat16),
            pltpu.VMEM((4 * BOX_DEV, devices), jnp.float32),
            pltpu.SemaphoreType.DMA,
        ],
        compiler_params=pltpu.CompilerParams(vmem_limit_bytes=32 * MIB),
        name="gather_rows",
    )(ends, *swept_from, cells, weights)


def swapped(blocks):
    return lax.all_to_all(blocks, AXES, split_axis=0, concat_axis=0, tiled=True)


def body(
    sensitivity,
    node_weight,
    dest_device,
    dest_cell,
    box_owner,
    box_slot,
    stiffness,
    anchor,
    coupling,
):
    devices = lax.axis_size("gx") * lax.axis_size("gy")
    count = sensitivity.shape[1]
    size_x, size_y, size_z = stiffness.shape
    lane = lambda values: values.reshape(1, count)
    rows = pack(
        devices,
        sensitivity,
        lane(node_weight),
        lane(dest_device),
        lane(dest_cell),
        lane(box_owner),
        lane(box_slot),
    )
    rows = swapped(rows)
    planes = [rows[:, p].reshape(-1) for p in range(6)]
    found = (planes[3].astype(jnp.int32) - CELL_SHIFT) << KEY_BITS
    keys = jnp.maximum(found + planes[5].astype(jnp.int32), -1)
    ordered = lax.sort((keys, *planes[:3], planes[4]), num_keys=1, is_stable=False)
    cells, *values, weights = [part.reshape(-1, 128) for part in ordered]
    blocks = cells.reshape(-1, STEP_ROWS // 128, 128)
    ends = jnp.stack([blocks[:, 0, 0], blocks[:, -1, -1]]) >> KEY_BITS
    fixed, faces = scatter(ends, cells, values, stiffness, anchor, coupling)
    field = fixed[0]
    for turn in range(1, SWEEPS - 1):
        field, *faces = sweep(*fixed, field, *exchange(*faces))
    swept_from = (*fixed, field, *exchange(*faces))
    field, partial = gather(ends, swept_from, cells, weights, devices)
    field = field.reshape(3, size_x, size_y, size_z)
    summed = jnp.sum(swapped(partial), axis=0).reshape(4, BOX_DEV)
    return (field, summed[:3])


def solution(mesh):
    placed = (
        P(None, AXES),
        P(AXES),
        P(AXES, None),
        P(AXES),
        P(AXES, None),
        P(AXES),
        P("gx", "gy", None),
        P(None, "gx", "gy", None),
        P(None, "gx", "gy", None),
    )
    return jax.shard_map(
        body,
        mesh=mesh,
        in_specs=placed,
        out_specs=(P(None, "gx", "gy", None), P(None, AXES)),
        check_vma=False,
    )
```

```python
import jax
import jax.numpy as jnp
from jax import lax
from jax.experimental import pallas as pl
from jax.experimental.pallas import tpu as pltpu
from jax.sharding import PartitionSpec as P

BOX_DEV = 64
BOX_BITS = 6
SWEEPS = 4
AXES = ("gx", "gy")
STEP_ROWS = 512
RANK_ROWS = 256
WINDOW = 32
SIDE = 8
PARTS = 4
CELL_SHIFT = 257
KEY_BITS = 13
MIB = 1024 * 1024


def dot_last(left, right):
    return lax.dot_general(
        left, right, (((1,), (1,)), ((), ())), preferred_element_type=jnp.float32
    )


def halves(values):
    high = values.astype(jnp.bfloat16).astype(jnp.float32)
    return high, values - high


def places(height, width):
    return lax.broadcasted_iota(jnp.int32, (height, width), 0)


def marked(mask, row):
    return jnp.where(mask, row, 0.0).astype(jnp.bfloat16)


def pack_kernel(*refs):
    given, rows, kept = refs[:6], refs[6], refs[7:13]
    ranks, upper, left, right, total, arrivals = refs[13:]
    sens, weight, device, cell, owner, slot = kept
    devices, _, capacity = rows.shape
    half = capacity // 2
    part = upper.shape[0]
    step = STEP_ROWS
    steps = sens.shape[1] // step
    copies = [
        pltpu.make_async_copy(given[p], kept[p], arrivals.at[p]) for p in range(len(given))
    ]
    for copy in copies:
        copy.start()
    before = lax.broadcasted_iota(jnp.int32, (part, part), 0)
    after = lax.broadcasted_iota(jnp.int32, (part, part), 1)
    upper[...] = marked(before < after, 1.0)
    total[...] = jnp.zeros_like(total)
    for copy in copies:
        copy.wait()

    def rank(i, base):
        for b in range(4):
            at = pl.ds(pl.multiple_of((i * 4 + b) * part, part), part)
            here = places(devices, part) == device[:, at]
            ones = jnp.where(here, 1.0, 0.0)
            within = jnp.dot(
                ones.astype(jnp.bfloat16), upper[...], preferred_element_type=jnp.float32
            )
            ranks[:, at] = jnp.sum(
                jnp.where(here, within + base, 0.0), axis=0, keepdims=True
            ).astype(jnp.int32)
            base = base + jnp.sum(ones, axis=1, keepdims=True)
        return base

    lax.fori_loop(0, sens.shape[1] // part // 4, rank, jnp.zeros((devices, 1), jnp.float32))

    def chunk(i, _):
        for b in range(4):
            at = pl.ds(pl.multiple_of((i * 4 + b) * step, step), step)
            rank = ranks[:, at]
            lane = device[:, at] + jnp.where(rank >= half, devices, 0)
            ones = marked(places(2 * devices, step) == lane, 1.0)
            left[b, :, :step] = ones
            left[b, :, step:] = ones
            here = places(half, step) == (rank & (half - 1))
            own_cell = cell[:, at]
            pairs = [halves(sens[k : k + 1, at]) for k in range(3)]
            pairs.append(
                (
                    (((own_cell >> 9) + 1) << 9).astype(jnp.float32),
                    ((own_cell & 511) + (CELL_SHIFT - 512)).astype(jnp.float32),
                )
            )
            pairs.append(halves(weight[:, at]))
            pairs.append(
                ((owner[:, at] * BOX_DEV).astype(jnp.float32), slot[:, at].astype(jnp.float32))
            )
            for p, (high, low) in enumerate(pairs):
                band = slice(p * half, (p + 1) * half)
                right[b, band, :step] = marked(here, high)
                right[b, band, step:] = marked(here, low)
        total[...] += sum(dot_last(right[b], left[b]) for b in range(4))
        return 0

    lax.fori_loop(0, steps // 4, chunk, 0)
    for p in range(6):
        band = total[p * half : (p + 1) * half, :]
        rows[:, p, :] = jnp.concatenate([band[:, :devices].T, band[:, devices:].T], axis=1)
    for p in range(6, 8):
        rows[:, p, :] = jnp.zeros((devices, capacity), jnp.float32)


def pack(devices, *given):
    count = given[0].shape[1]
    capacity = 2 * count // devices
    return pl.pallas_call(
        pack_kernel,
        in_specs=[pl.BlockSpec(memory_space=pltpu.HBM)] * len(given),
        out_shape=jax.ShapeDtypeStruct((devices, 8, capacity), jnp.float32),
        scratch_shapes=[pltpu.VMEM(part.shape, part.dtype) for part in given]
        + [
            pltpu.VMEM((1, count), jnp.int32),
            pltpu.VMEM((RANK_ROWS, RANK_ROWS), jnp.bfloat16),
            pltpu.VMEM((4, 2 * devices, 2 * STEP_ROWS), jnp.bfloat16),
            pltpu.VMEM((4, 3 * capacity, 2 * STEP_ROWS), jnp.bfloat16),
            pltpu.VMEM((3 * capacity, 2 * devices), jnp.float32),
            pltpu.SemaphoreType.DMA((len(given),)),
        ],
        compiler_params=pltpu.CompilerParams(vmem_limit_bytes=58 * MIB),
        name="pack_rows",
    )(*given)


def windows(ends, i):
    first = jnp.maximum(ends[0, i] >> 8, 0)
    start = first & ~7
    return start, (jnp.maximum((ends[1, i] >> 8) + WINDOW - start, 0)) // WINDOW


def filled(ends):
    groups = ends.shape[1] // SIDE

    def count(g, empty):
        return empty + jnp.where(ends[1, g * SIDE + SIDE - 1] < 0, 1, 0)

    return lax.fori_loop(0, groups, count, 0)


def scatter_kernel(*refs):
    ends, cells, one, two, three, stiff_at, anchor_at, coupling_at = refs[:8]
    load, scaled, inverse, stiff, head_x, tail_x, head_y, tail_y = refs[8:16]
    anchor, coupling, left, right, arrivals = refs[16:]
    copies = [
        pltpu.make_async_copy(source, target, arrivals.at[p])
        for p, (source, target) in enumerate(
            ((stiff_at, stiff), (anchor_at, anchor), (coupling_at, coupling))
        )
    ]
    for copy in copies:
        copy.start()
    height, depth = load.shape[1:]
    lines, width = cells.shape
    part = depth // PARTS
    group = STEP_ROWS // width
    step = STEP_ROWS
    load[...] = jnp.zeros_like(load)

    def fill(i, b):
        for q in range(group):
            row = pl.ds(i * group + q, 1)
            there = places(part, width) == ((cells[row, :] >> KEY_BITS) & (part - 1))
            for k, sens in enumerate((one, two, three)):
                high, low = halves(sens[row, :])
                band = slice(k * part, (k + 1) * part)
                right[b, band, q * width : (q + 1) * width] = marked(there, high)
                right[b, band, step + q * width : step + (q + 1) * width] = marked(there, low)

    def window(i, b, start, w):
        least = start + w * WINDOW
        base = pl.multiple_of(jnp.minimum(least, height - WINDOW), 8)
        for q in range(group):
            cell = cells[pl.ds(i * group + q, 1), :] >> KEY_BITS
            place = window_place(cell, least, base, PARTS)
            hot = marked(places(PARTS * WINDOW, width) == place, 1.0)
            left[b, :, q * width : (q + 1) * width] = hot
            left[b, :, step + q * width : step + (q + 1) * width] = hot
        sums = dot_last(left[b], right[b])

        def add():
            for k in range(3):
                for side in range(PARTS // 2):
                    at = (k, pl.ds(base, WINDOW), slice(side * 2 * part, (side + 1) * 2 * part))
                    load[at] += jnp.concatenate(
                        [
                            sums[p * WINDOW : (p + 1) * WINDOW, k * part : (k + 1) * part]
                            for p in (2 * side, 2 * side + 1)
                        ],
                        axis=1,
                    )

        return add

    def chunks(i, _):
        own = [i * SIDE + b for b in range(SIDE)]
        spans = [windows(ends, j) for j in own]
        for b in range(SIDE):
            fill(own[b], b)
        adds = [window(own[b], b, spans[b][0], 0) for b in range(SIDE)]
        for add in adds:
            add()
        for b in range(SIDE):

            def more(w, _, b=b):
                window(own[b], b, spans[b][0], w)()
                return 0

            lax.fori_loop(1, spans[b][1], more, 0)
        return 0

    lax.fori_loop(filled(ends), lines // group // SIDE, chunks, 0)
    for copy in copies:
        copy.wait()
    size_x, size_y = head_y.shape[1], head_x.shape[1]
    for x in range(size_x):
        at = slice(x * size_y, (x + 1) * size_y)
        weight = stiff[at]
        for k in range(3):
            own = 1.0 / (6.0 * weight + anchor[k, at] + coupling[4 * k, at])
            inverse[k, at] = own
            for place, j in enumerate(others(k)):
                scaled[2 * k + place, at] = coupling[3 * j + k, at] * own
            fresh = load[k, at] * own
            load[k, at] = fresh
            moved = weight * fresh
            if x == 0:
                head_x[k] = moved
            if x == size_x - 1:
                tail_x[k] = moved
            head_y[k, x : x + 1] = moved[:1]
            tail_y[k, x : x + 1] = moved[size_y - 1 :]


def window_place(cell, least, base, parts):
    line = cell >> 8
    place = ((cell & 255) * parts >> 8) * WINDOW + line - base
    inside = (line >= least) & (line < base + WINDOW)
    return jnp.where(inside, place, -1)


def scatter(ends, cells, values, stiff, anchor, coupling):
    size_x, size_y, depth = stiff.shape
    height = size_x * size_y
    vmem = pl.BlockSpec(memory_space=pltpu.VMEM)
    shapes = [(3, height, depth), (6, height, depth), (3, height, depth), (height, depth)]
    shapes += [(3, size_y, depth)] * 2 + [(3, size_x, depth)] * 2
    outs = pl.pallas_call(
        scatter_kernel,
        in_specs=[pl.BlockSpec(memory_space=pltpu.SMEM)]
        + [vmem] * 4
        + [pl.BlockSpec(memory_space=pltpu.HBM)] * 3,
        out_specs=[vmem] * 8,
        out_shape=[jax.ShapeDtypeStruct(shape, jnp.float32) for shape in shapes],
        scratch_shapes=[
            pltpu.VMEM((3, height, depth), jnp.float32),
            pltpu.VMEM((9, height, depth), jnp.float32),
            pltpu.VMEM((SIDE, PARTS * WINDOW, 2 * STEP_ROWS), jnp.bfloat16),
            pltpu.VMEM((SIDE, 3 * depth // PARTS, 2 * STEP_ROWS), jnp.bfloat16),
            pltpu.SemaphoreType.DMA((3,)),
        ],
        compiler_params=pltpu.CompilerParams(vmem_limit_bytes=41 * MIB),
        name="scatter_rows",
    )(
        ends,
        cells,
        *values,
        *(part.reshape(*part.shape[:-3], height, depth) for part in (stiff, anchor, coupling)),
    )
    cells_of = [part.reshape(*part.shape[:-2], size_x, size_y, depth) for part in outs[:4]]
    return cells_of, outs[4:]


def swept(first, scaled, inverse, stiff, field, halo, padded, store):
    _, size_x, size_y, size_z = field.shape
    south, north, west, east = halo
    padded[:, 0] = west[...]
    padded[:, size_x + 1] = east[...]
    for x in range(size_x):
        for k in range(3):
            padded[k, x + 1] = stiff[x] * field[k, x]
    row = lax.broadcasted_iota(jnp.int32, (size_y, size_z), 0)
    column = lax.broadcasted_iota(jnp.int32, (size_y, size_z), 1)
    for x in range(size_x):
        own = [field[k, x] for k in range(3)]
        for k in range(3):
            middle = padded[k, x + 1]
            total = padded[k, x] + padded[k, x + 2]
            total = total + jnp.where(row == 0, south[k, x : x + 1], pltpu.roll(middle, 1, 0))
            total = total + jnp.where(
                row == size_y - 1, north[k, x : x + 1], pltpu.roll(middle, size_y - 1, 0)
            )
            total = total + jnp.where(column == 0, 0.0, pltpu.roll(middle, 1, 1))
            total = total + jnp.where(
                column == size_z - 1, 0.0, pltpu.roll(middle, size_z - 1, 1)
            )
            fresh = first[k, x] + total * inverse[k, x]
            for place, j in enumerate(others(k)):
                fresh = fresh - scaled[2 * k + place, x] * own[j]
            store(k, x, fresh)


def others(k):
    return [j for j in range(3) if j != k]


def sweep_kernel(first, scaled, inverse, stiff, field, south, north, west, east, *outs):
    result, head_x, tail_x, head_y, tail_y, padded = outs
    size_x, size_y = field.shape[1:3]

    def store(k, x, fresh):
        result[k, x] = fresh
        moved = stiff[x] * fresh
        if x == 0:
            head_x[k] = moved
        if x == size_x - 1:
            tail_x[k] = moved
        head_y[k, x : x + 1] = moved[:1]
        tail_y[k, x : x + 1] = moved[size_y - 1 :]

    swept(first, scaled, inverse, stiff, field, (south, north, west, east), padded, store)


def sweep(*given):
    _, size_x, size_y, size_z = given[0].shape
    shapes = [given[0].shape] + [(3, size_y, size_z)] * 2 + [(3, size_x, size_z)] * 2
    return pl.pallas_call(
        sweep_kernel,
        out_shape=[jax.ShapeDtypeStruct(shape, jnp.float32) for shape in shapes],
        scratch_shapes=[pltpu.VMEM((3, size_x + 2, size_y, size_z), jnp.float32)],
        compiler_params=pltpu.CompilerParams(vmem_limit_bytes=8 * MIB),
        name="sweep_cells",
    )(*given)


def exchange(head_x, tail_x, head_y, tail_y):
    def shifted(face, axis, up):
        pairs = [(i, i + 1) if up else (i + 1, i) for i in range(lax.axis_size(axis) - 1)]
        return lax.ppermute(face, axis, pairs)

    south = shifted(tail_y, "gy", True)
    north = shifted(head_y, "gy", False)
    west = shifted(tail_x, "gx", True)
    east = shifted(head_x, "gx", False)
    return south, north, west, east


def gather_kernel(*refs):
    ends, first, scaled, inverse, stiff, before, south, north, west, east = refs[:10]
    cells, weights, final, sums, padded, field, hot, left, right, total, sent = refs[10:]
    size_y = before.shape[2]

    def store(k, x, fresh):
        field[k, x * size_y : (x + 1) * size_y] = fresh

    swept(first, scaled, inverse, stiff, before, (south, north, west, east), padded, store)
    out = pltpu.make_async_copy(field, final, sent)
    out.start()
    height, depth = field.shape[1:]
    lines, width = cells.shape
    half = depth // 2
    group = STEP_ROWS // width
    step = STEP_ROWS
    total[...] = jnp.zeros_like(total)

    def rows(i):
        return [pl.ds(i * group + q, 1) for q in range(group)]

    def fill(i, b):
        for q, row in enumerate(rows(i)):
            place = (cells[row, :] >> KEY_BITS) & (half - 1)
            ones = marked(places(half, width) == place, 1.0)
            hot[b, :half, q * width : (q + 1) * width] = ones
            hot[b, half:, q * width : (q + 1) * width] = ones

    def window(i, b, start, w):
        least = start + w * WINDOW
        base = pl.multiple_of(jnp.minimum(least, height - WINDOW), 8)
        there = [
            places(2 * WINDOW, width)
            == window_place(cells[row, :] >> KEY_BITS, least, base, 2)
            for row in rows(i)
        ]
        block = jnp.concatenate(
            [
                field[k, pl.ds(base, WINDOW), side * half : (side + 1) * half]
                for k in range(3)
                for side in range(2)
            ],
            axis=0,
        )
        both = jnp.concatenate(halves(block), axis=1).astype(jnp.bfloat16)
        parts = jnp.dot(both, hot[b], preferred_element_type=jnp.float32)
        picked = []
        for k in range(3):
            part = parts[k * 2 * WINDOW : (k + 1) * 2 * WINDOW]
            picked.append(
                jnp.concatenate(
                    [
                        jnp.sum(
                            jnp.where(there[q], part[:, q * width : (q + 1) * width], 0.0),
                            axis=0,
                            keepdims=True,
                        )
                        for q in range(group)
                    ],
                    axis=1,
                )
            )
        return tuple(picked)

    def spread(i, b, picked):
        for q, row in enumerate(rows(i)):
            at = slice(q * width, (q + 1) * width)
            low_at = slice(step + q * width, step + (q + 1) * width)
            weight = weights[row, :]
            box = cells[row, :] & (2**KEY_BITS - 1)
            owned = marked(places(left.shape[1], width) == (box >> BOX_BITS), 1.0)
            left[b, :, at] = owned
            left[b, :, low_at] = owned
            inside = places(BOX_DEV, width) == (box & (BOX_DEV - 1))
            for k in range(3):
                high, low = halves(picked[k][:, at] * weight)
                band = slice(k * BOX_DEV, (k + 1) * BOX_DEV)
                right[b, band, at] = marked(inside, high)
                right[b, band, low_at] = marked(inside, low)

    def chunks(i, _):
        own = [i * SIDE + b for b in range(SIDE)]
        spans = [windows(ends, j) for j in own]
        for b in range(SIDE):
            fill(own[b], b)
        firsts = [window(own[b], b, spans[b][0], 0) for b in range(SIDE)]
        finals = []
        for b in range(SIDE):

            def more(w, picked, b=b):
                fresh = window(own[b], b, spans[b][0], w)
                return tuple(old + new for old, new in zip(picked, fresh))

            finals.append(lax.fori_loop(1, spans[b][1], more, firsts[b]))
        for b in range(SIDE):
            spread(own[b], b, finals[b])
        parts = [dot_last(right[b], left[b]) for b in range(SIDE)]
        total[: 3 * BOX_DEV, :] += sum(parts[1:], parts[0])
        return 0

    lax.fori_loop(filled(ends), lines // group // SIDE, chunks, 0)
    for p in range(2):
        sums[:, p, :] = total[p * 128 : (p + 1) * 128, :].T
    out.wait()


def gather(ends, swept_from, cells, weights, devices):
    _, size_x, size_y, depth = swept_from[0].shape
    cube = (3, size_x * size_y, depth)
    vmem = pl.BlockSpec(memory_space=pltpu.VMEM)
    return pl.pallas_call(
        gather_kernel,
        in_specs=[pl.BlockSpec(memory_space=pltpu.SMEM)] + [vmem] * (len(swept_from) + 2),
        out_specs=[pl.BlockSpec(memory_space=pltpu.HBM), vmem],
        out_shape=[
            jax.ShapeDtypeStruct(cube, jnp.float32),
            jax.ShapeDtypeStruct((devices, 2, 128), jnp.float32),
        ],
        scratch_shapes=[
            pltpu.VMEM((3, size_x + 2, size_y, depth), jnp.float32),
            pltpu.VMEM(cube, jnp.float32),
            pltpu.VMEM((SIDE, depth, STEP_ROWS), jnp.bfloat16),
            pltpu.VMEM((SIDE, devices, 2 * STEP_ROWS), jnp.bfloat16),
            pltpu.VMEM((SIDE, 3 * BOX_DEV, 2 * STEP_ROWS), jnp.bfloat16),
            pltpu.VMEM((4 * BOX_DEV, devices), jnp.float32),
            pltpu.SemaphoreType.DMA,
        ],
        compiler_params=pltpu.CompilerParams(vmem_limit_bytes=32 * MIB),
        name="gather_rows",
    )(ends, *swept_from, cells, weights)


def swapped(blocks):
    return lax.all_to_all(blocks, AXES, split_axis=0, concat_axis=0, tiled=True)


def body(
    sensitivity,
    node_weight,
    dest_device,
    dest_cell,
    box_owner,
    box_slot,
    stiffness,
    anchor,
    coupling,
):
    devices = lax.axis_size("gx") * lax.axis_size("gy")
    count = sensitivity.shape[1]
    size_x, size_y, size_z = stiffness.shape
    lane = lambda values: values.reshape(1, count)
    rows = pack(
        devices,
        sensitivity,
        lane(node_weight),
        lane(dest_device),
        lane(dest_cell),
        lane(box_owner),
        lane(box_slot),
    )
    rows = swapped(rows)
    planes = [rows[:, p].reshape(-1) for p in range(6)]
    found = (planes[3].astype(jnp.int32) - CELL_SHIFT) << KEY_BITS
    keys = jnp.maximum(found + planes[5].astype(jnp.int32), -1)
    ordered = lax.sort((keys, *planes[:3], planes[4]), num_keys=1, is_stable=False)
    cells, *values, weights = [part.reshape(-1, 128) for part in ordered]
    blocks = cells.reshape(-1, STEP_ROWS // 128, 128)
    ends = jnp.stack([blocks[:, 0, 0], blocks[:, -1, -1]]) >> KEY_BITS
    fixed, faces = scatter(ends, cells, values, stiffness, anchor, coupling)
    field = fixed[0]
    for turn in range(1, SWEEPS - 1):
        field, *faces = sweep(*fixed, field, *exchange(*faces))
    swept_from = (*fixed, field, *exchange(*faces))
    field, partial = gather(ends, swept_from, cells, weights, devices)
    field = field.reshape(3, size_x, size_y, size_z)
    summed = jnp.sum(swapped(partial), axis=0).reshape(4, BOX_DEV)
    return (field, summed[:3])


def solution(mesh):
    placed = (
        P(None, AXES),
        P(AXES),
        P(AXES, None),
        P(AXES),
        P(AXES, None),
        P(AXES),
        P("gx", "gy", None),
        P(None, "gx", "gy", None),
        P(None, "gx", "gy", None),
    )
    return jax.shard_map(
        body,
        mesh=mesh,
        in_specs=placed,
        out_specs=(P(None, "gx", "gy", None), P(None, AXES)),
        check_vma=False,
    )
```
